768 devices in a mesh: gx: 96 (over y_hi, z, core), yz: 8 (over y_lo, x).
Axes of the slice: x: 4, y: 8 (y_hi: 4, y_lo: 2; y = y_hi * 2 + y_lo), z: 12, core: 2. Of those that a mesh axis runs over, the one named last changes fastest.
Arguments:
- right_side: float32 [384, 256, 512], P('gx', 'yz'), may hold values from -36 to 36
- potential: float32 [384, 256, 512], P('gx', 'yz'), may hold values from -3 to 3
- permittivity: float32 [384, 256, 512], P('gx', 'yz'), may hold values from 0.1 to 4
- ion_mask: int32 [384, 256, 512], P('gx', 'yz'), may hold values 0 or 1
Outputs:
- solution_field: float32 [384, 256, 512], P('gx', 'yz')
- residual: float32 [384, 256, 512], P('gx', 'yz')
The draws below stay inside these ranges and needn't reach their ends.
All inputs are finite; a program needn't handle non-finite values. No bound on the sum of `ion_mask` on one device may be relied on, other than what follows from the above.
Results may differ from the reference program's by a relative error of at most 0.03.
Values sent between devices are 32-bit elements; how exact they have to be, the bound alone decides.
A program may use at most 32 MiB of HBM per device.

```python
import math
import jax
import jax.numpy as jnp

NX = 384
NY = 256
NZ = 512


def draw_right_side(key, part):
    key = jax.random.fold_in(key, 11)
    first, second = jax.random.split(key)
    rough = jnp.exp(jax.random.uniform(second, (NX, NY, NZ), jnp.float32) * jnp.log(10.0))
    xline = jnp.arange(NX, dtype=jnp.float32) / max(NX - 1, 1)
    yline = jnp.arange(NY, dtype=jnp.float32) / max(NY - 1, 1)
    ramp = (1.0 + 2.0 * xline)[:, None, None] * (1.0 + 2.0 * yline)[None, :, None]
    base = jnp.clip(jax.random.normal(first, (NX, NY, NZ), jnp.float32), -4.0, 4.0)
    return (0.1 * base * rough * ramp).astype(jnp.float32)


def touch_ends(result, rng, least, largest):
    longest = result.shape.index(max(result.shape))
    spots = []
    for shift in (0, 1):
        where = [jax.random.randint(jax.random.fold_in(rng, axis), (), 0, length) for axis, length in enumerate(result.shape)]
        where[longest] = (where[longest] + shift) % result.shape[longest]
        spots.append(tuple(where))
    return result.at[spots[0]].set(least).at[spots[1]].set(largest)


def levels(own_key, extent, cuts, low, high):
    factor_of = 1.0
    for dim, blocks in cuts:
        draws = jax.random.uniform(jax.random.fold_in(jax.random.fold_in(own_key, 6), dim), (blocks,), jnp.float32, low / len(cuts), high / len(cuts))
        factor_of = factor_of * jnp.repeat(jnp.exp(draws), extent[dim] // blocks).reshape((-1,) + (1,) * (len(extent) - 1 - dim))
    return factor_of


def normal_values(key, shape, scale, limit, shards=(), kind=jnp.bfloat16):
    factor_of = levels(key, shape, shards, -0.22, 0.18) if shards else 1.0
    array = jax.random.normal(key, shape, jnp.float32) * scale * factor_of
    return jnp.minimum(jnp.maximum(array, -limit), limit).astype(kind)


def setup_inputs(seed: int = 0) -> dict:
    key_of = jax.random.split(jax.random.key(seed), 5)
    right_side = draw_right_side(jax.random.fold_in(key_of[4], 71), 0)
    potential = normal_values(key_of[1], (NX, NY, NZ), 1.0, 3.0, ((0, 96), (1, 8)), jnp.float32)
    permittivity = jnp.clip(jnp.exp(math.log(4.0) - 3.6888794 * jax.random.uniform(key_of[2], (NX, NY, NZ), jnp.float32) ** levels(key_of[2], (NX, NY, NZ), ((0, 96), (1, 8)), -0.2, 0.2)), 0.1, 4.0)
    ion_mask = touch_ends((jax.random.randint(key_of[3], (NX, NY, NZ), 0, 4) < 3).astype(jnp.int32), jax.random.fold_in(key_of[3], 1), 0, 1)
    return dict(right_side=right_side, potential=potential, permittivity=permittivity, ion_mask=ion_mask)


def six_sides(padded):
    return [padded[2:, 1:-1, 1:-1], padded[:-2, 1:-1, 1:-1],
            padded[1:-1, 2:, 1:-1], padded[1:-1, :-2, 1:-1],
            padded[1:-1, 1:-1, 2:], padded[1:-1, 1:-1, :-2]]


def reference(right_side, potential, permittivity, ion_mask):
    eps = permittivity
    sides = six_sides(jnp.pad(eps, 1))
    faces = [jnp.where(other > 0, 2.0 * eps * other / (eps + other), eps) for other in sides]
    ionic = 0.5 * ion_mask.astype(jnp.float32) * jnp.cosh(potential)
    diag = ionic + faces[0] + faces[1] + faces[2] + faces[3] + faces[4] + faces[5]

    def operate(field):
        near = six_sides(jnp.pad(field, 1))
        total = diag * field
        for face, other in zip(faces, near):
            total = total - face * other
        return total

    solution_field = jnp.zeros_like(right_side)
    residual = right_side
    scaled = residual / diag
    direction = scaled
    rz_now = jnp.sum(residual * scaled)
    for step in range(2):
        image = operate(direction)
        alpha = rz_now / jnp.sum(direction * image)
        solution_field = solution_field + alpha * direction
        residual = residual - alpha * image
        if step < 1:
            scaled = residual / diag
            rz_next = jnp.sum(residual * scaled)
            direction = scaled + (rz_next / rz_now) * direction
            rz_now = rz_next
    return solution_field, residual
```

```python
import functools

import jax
import jax.numpy as jnp
from jax import lax
from jax.experimental import pallas as pl
from jax.experimental.pallas import tpu as pltpu
from jax.sharding import PartitionSpec as P

MESH = pl.DeviceIdType.MESH
SIZES = dict(y_hi=4, z=12, core=2, y_lo=2, x=4)


def face(a, b):
    return (2.0 * a * b) / (a + b)


def kernel(sizes, b_hbm, p_hbm, e_hbm, m_hbm, x_out, r_out,
           B, PT, E, M, CX, CXE, CY, CYE, CZ, D, RD, Z, Q, U, W, XO, RO,
           XR, YR, YS, part, sums, g0, g1, g2,
           in_sem, out_sem, hs_sem, hr_sem, as_sem, ar_sem):
    nyh, nz, nc, nyl, nx = (sizes[k] for k in ("y_hi", "z", "core", "y_lo", "x"))
    ngx, nyz = nyh * nz * nc, nyl * nx
    gx, yz = lax.axis_index("gx"), lax.axis_index("yz")
    core, zz, yh = gx % nc, (gx // nc) % nz, gx // (nc * nz)
    xx, yl = yz % nx, yz // nx
    ny = nyh * nyl
    yy = yh * nyl + yl
    planes, rows, lanes = E.shape
    tiles = rows // 8

    left = ((gx + ngx - 1) % ngx, yz)
    right = ((gx + 1) % ngx, yz)
    down = (gx, (yz + nyz - 1) % nyz)
    up = (gx, (yz + 1) % nyz)
    near = (left, right, down, up)

    def place(yh_, z_, c_, yl_, x_):
        return ((yh_ * nz + z_) * nc + c_, yl_ * nx + x_)

    na = nx * nc
    ia = xx * nc + core
    group_a = [place(yh, zz, ((ia + d) % na) % nc, yl, ((ia + d) % na) // nc) for d in range(1, na)]
    group_b = [place(((yy + d) % ny) // nyl, zz, core, ((yy + d) % ny) % nyl, xx) for d in range(1, ny)]
    group_c = [place(yh, (zz + d) % nz, core, yl, xx) for d in range(1, nz)]
    groups = (group_a, group_b, group_c)

    barrier = pltpu.get_barrier_semaphore()
    count = 0
    for peer in near + tuple(group_a) + tuple(group_b) + tuple(group_c):
        pl.semaphore_signal(barrier, inc=1, device_id=peer, device_id_type=MESH)
        count += 1

    loads = [pltpu.make_async_copy(s, d, in_sem.at[i])
             for i, (s, d) in enumerate(((e_hbm, E), (p_hbm, PT), (m_hbm, M), (b_hbm, B)))]
    for c in loads:
        c.start()

    x_lo, x_hi = gx > 0, gx < ngx - 1
    y_lo, y_hi = yz > 0, yz < nyz - 1
    lane = lax.broadcasted_iota(jnp.int32, (8, lanes), 1)
    sub = lax.broadcasted_iota(jnp.int32, (8, lanes), 0)

    def at(j):
        return slice(8 * j, 8 * j + 8)

    def before(ref, p, j):
        if j == 0:
            return pltpu.roll(ref[p, at(0), :], 1, 0)
        return ref[p, 8 * j - 1:8 * j + 7, :]

    def after(ref, p, j):
        if j == tiles - 1:
            return pltpu.roll(ref[p, at(j), :], 7, 0)
        return ref[p, 8 * j + 1:8 * j + 9, :]

    def exchange(n, field):
        copies = []
        for k, (src, dst, dev) in enumerate((
                (YS.at[n, 0], YR.at[n, 1], down), (YS.at[n, 1], YR.at[n, 0], up),
                (field.at[0], XR.at[n, 1], left), (field.at[planes - 1], XR.at[n, 0], right))):
            c = pltpu.make_async_remote_copy(src_ref=src, dst_ref=dst, send_sem=hs_sem.at[n, k],
                                             recv_sem=hr_sem.at[n, k], device_id=dev, device_id_type=MESH)
            c.start()
            copies.append(c)
        return copies

    loads[0].wait()
    YS[0, 0] = E[:, 0, :]
    YS[0, 1] = E[:, rows - 1, :]
    pl.semaphore_wait(barrier, count)
    sent = exchange(0, E)

    CY[:, rows:rows + 8, :] = jnp.zeros((planes, 8, lanes), jnp.float32)
    for p in range(planes):
        for j in range(tiles):
            e = E[p, at(j), :]
            CZ[p, at(j), :] = jnp.where(lane == lanes - 1, 0.0, face(e, pltpu.roll(e, lanes - 1, 1)))
            cy = face(e, before(E, p, j))
            CY[p, at(j), :] = jnp.where(sub == 0, 0.0, cy) if j == 0 else cy
            if p < planes - 1:
                CX[p, at(j), :] = face(e, E[p + 1, at(j), :])
    loads[1].wait()
    loads[2].wait()
    for p in range(planes):
        for j in range(tiles):
            e, cz = E[p, at(j), :], CZ[p, at(j), :]
            pt = PT[p, at(j), :]
            d = 0.25 * M[p, at(j), :].astype(jnp.float32) * (jnp.exp(pt) + jnp.exp(-pt))
            d = d + cz + pltpu.roll(cz, 1, 1) + jnp.where((lane == 0) | (lane == lanes - 1), e, 0.0)
            d = d + CY[p, at(j), :] + CY[p, 8 * j + 1:8 * j + 9, :]
            if p > 0:
                d = d + CX[p - 1, at(j), :]
            if p < planes - 1:
                d = d + CX[p, at(j), :]
            D[p, at(j), :] = d

    loads[3].wait()
    for c in sent:
        c.wait_recv()
    for k, row, inside in ((0, 0, y_lo), (1, rows - 1, y_hi)):
        e = E[:, row, :]
        n = jnp.where(inside, YR[0, k], 0.0)
        c = face(e, n)
        CYE[k] = c
        D[:, row, :] = D[:, row, :] + jnp.where(inside, c, e)
    for k, p, inside in ((0, 0, x_lo), (1, planes - 1, x_hi)):
        for j in range(tiles):
            e = E[p, at(j), :]
            n = jnp.where(inside, XR[0, k, at(j), :], 0.0)
            c = face(e, n)
            CXE[k, at(j), :] = c
            d = D[p, at(j), :] + jnp.where(inside, c, e)
            rd = 1.0 / d
            D[p, at(j), :] = d
            RD[p, at(j), :] = rd
            Z[p, at(j), :] = B[p, at(j), :] * rd
    for p in range(1, planes - 1):
        for j in range(tiles):
            rd = 1.0 / D[p, at(j), :]
            RD[p, at(j), :] = rd
            Z[p, at(j), :] = B[p, at(j), :] * rd
    YS[1, 0] = Z[:, 0, :]
    YS[1, 1] = Z[:, rows - 1, :]
    sent_z = exchange(1, Z)

    def image(V, p, j):
        v, cz = V[p, at(j), :], CZ[p, at(j), :]
        t = D[p, at(j), :] * v
        t = t - cz * pltpu.roll(v, lanes - 1, 1) - pltpu.roll(cz * v, 1, 1)
        t = t - CY[p, at(j), :] * before(V, p, j) - CY[p, 8 * j + 1:8 * j + 9, :] * after(V, p, j)
        if p > 0:
            t = t - CX[p - 1, at(j), :] * V[p - 1, at(j), :]
        if p < planes - 1:
            t = t - CX[p, at(j), :] * V[p + 1, at(j), :]
        return t

    for p in range(planes):
        for j in range(tiles):
            Q[p, at(j), :] = image(Z, p, j)
    for c in sent_z:
        c.wait_recv()
    for k, row in ((0, 0), (1, rows - 1)):
        Q[:, row, :] = Q[:, row, :] - CYE[k] * YR[1, k]
    for k, p in ((0, 0), (1, planes - 1)):
        for j in range(tiles):
            Q[p, at(j), :] = Q[p, at(j), :] - CXE[k, at(j), :] * XR[1, k, at(j), :]
    s0 = s1 = s2 = s3 = jnp.zeros((8, lanes), jnp.float32)
    for p in range(planes):
        for j in range(tiles):
            U[p, at(j), :] = Q[p, at(j), :] * RD[p, at(j), :]
    YS[2, 0] = U[:, 0, :]
    YS[2, 1] = U[:, rows - 1, :]
    sent_u = exchange(2, U)
    for p in range(planes):
        for j in range(tiles):
            z, q, u = Z[p, at(j), :], Q[p, at(j), :], U[p, at(j), :]
            w = image(U, p, j)
            W[p, at(j), :] = w
            s0 = s0 + B[p, at(j), :] * z
            s1 = s1 + z * q
            s2 = s2 + q * u
            s3 = s3 + u * w
    for c in sent_u:
        c.wait_recv()
    edge = jnp.zeros((planes, lanes), jnp.float32)
    for k, row in ((0, 0), (1, rows - 1)):
        t = CYE[k] * YR[2, k]
        edge = edge + U[:, row, :] * t
        W[:, row, :] = W[:, row, :] - t
    for k, p in ((0, 0), (1, planes - 1)):
        for j in range(tiles):
            t = CXE[k, at(j), :] * XR[2, k, at(j), :]
            s3 = s3 - U[p, at(j), :] * t
            W[p, at(j), :] = W[p, at(j), :] - t

    def folded(s):
        t = s[:, :128]
        for i in range(128, lanes, 128):
            t = t + s[:, i:i + 128]
        return jnp.sum(t, axis=0, keepdims=True)

    part[0, 0:1, :] = folded(s0)
    part[0, 1:2, :] = folded(s1)
    part[0, 2:3, :] = folded(s2)
    part[0, 3:4, :] = folded(s3) - folded(edge)
    sends = []
    for n, (peers, got) in enumerate(zip(groups, (g0, g1, g2))):
        size = len(peers)
        for d, peer in enumerate(peers):
            pltpu.make_async_remote_copy(src_ref=part.at[n], dst_ref=got.at[d], send_sem=as_sem.at[n],
                                         recv_sem=ar_sem.at[n], device_id=peer, device_id_type=MESH).start()
        total = part[n]
        if size:
            pltpu.make_async_copy(got, got, ar_sem.at[n]).wait()
            for d in range(size):
                total = total + got[d]
        part[n + 1] = total
    s = jnp.sum(part[3], axis=1, keepdims=True)
    s0, s1, s2, s3 = s[0:1], s[1:2], s[2:3], s[3:4]
    a, g, h = s0 / s1, s2 / s1, s3 / s1
    cu = (a * g - 1.0) / (h - g * g)
    cz = a + g * cu
    stores = []
    for p in range(planes):
        for j in range(tiles):
            XO[p, at(j), :] = cz * Z[p, at(j), :] - cu * U[p, at(j), :]
            RO[p, at(j), :] = B[p, at(j), :] - cz * Q[p, at(j), :] + cu * W[p, at(j), :]
        for i, (src, dst) in enumerate(((XO, x_out), (RO, r_out))):
            c = pltpu.make_async_copy(src.at[p], dst.at[p], out_sem.at[i, p])
            c.start()
            stores.append(c)
    for n, (peers, got) in enumerate(zip(groups, (g0, g1, g2))):
        if peers:
            pltpu.make_async_copy(got, got, as_sem.at[n]).wait()
    for c in sent + sent_z + sent_u:
        c.wait_send()
    for c in stores:
        c.wait()


def local(sizes, right_side, potential, permittivity, ion_mask):
    f32 = jnp.float32
    planes, rows, lanes = right_side.shape
    block = (planes, rows, lanes)
    groups = (sizes["x"] * sizes["core"], sizes["y_hi"] * sizes["y_lo"], sizes["z"])
    vm = lambda *s: pltpu.VMEM(s, f32)
    scratch = [
        vm(*block), vm(*block), vm(*block), pltpu.VMEM(block, jnp.int32),
        vm(planes - 1, rows, lanes), vm(2, rows, lanes), vm(planes, rows + 8, lanes), vm(2, planes, lanes), vm(*block),
        vm(*block), vm(*block), vm(*block), vm(*block), vm(*block), vm(*block), vm(*block), vm(*block),
        vm(3, 2, rows, lanes), vm(3, 2, planes, lanes), vm(3, 2, planes, lanes),
        vm(4, 4, 128), vm(4, 128),
    ] + [vm(max(n - 1, 1), 4, 128) for n in groups] + [
        pltpu.SemaphoreType.DMA((4,)), pltpu.SemaphoreType.DMA((2, planes)),
        pltpu.SemaphoreType.DMA((3, 4)), pltpu.SemaphoreType.DMA((3, 4)),
        pltpu.SemaphoreType.DMA((3,)), pltpu.SemaphoreType.DMA((3,)),
    ]
    any_ = pl.BlockSpec(memory_space=pl.ANY)
    return pl.pallas_call(
        functools.partial(kernel, sizes),
        out_shape=(jax.ShapeDtypeStruct(block, f32), jax.ShapeDtypeStruct(block, f32)),
        in_specs=[any_] * 4,
        out_specs=(any_, any_),
        scratch_shapes=scratch,
        compiler_params=pltpu.CompilerParams(collective_id=0, has_side_effects=True, vmem_limit_bytes=32 * 2**20),
    )(right_side, potential, permittivity, ion_mask)


def solution(mesh, sizes=SIZES):
    spec = P("gx", "yz", None)
    return jax.shard_map(functools.partial(local, sizes), mesh=mesh, in_specs=(spec,) * 4, out_specs=(spec,) * 2,
                         check_vma=False)
```

```python
import functools

import jax
import jax.numpy as jnp
from jax import lax
from jax.experimental import pallas as pl
from jax.experimental.pallas import tpu as pltpu
from jax.sharding import PartitionSpec as P

MESH = pl.DeviceIdType.MESH
SIZES = dict(y_hi=4, z=12, core=2, y_lo=2, x=4)


def face(a, b):
    return (2.0 * a * b) / (a + b)


def kernel(sizes, b_hbm, p_hbm, e_hbm, m_hbm, B, Z, U, Q, W, coef,
           PT, E, M, CX, CXE, CY, CZ, D0, D, RD, TS,
           XB, RB, YB, GB, RS, YS, GS, EX, T2, T4, CYH, CZH, ZH, RH, UH, ADD, CY1, Z1, R1, N1, PZ, PU,
           part, g0, g1, in_sem, hs_sem, hr_sem, as_sem, ar_sem, here):
    nyh, nz, nc, nyl, nx = (sizes[k] for k in ("y_hi", "z", "core", "y_lo", "x"))
    ngx, nyz = nyh * nz * nc, nyl * nx
    gx, yz = lax.axis_index("gx"), lax.axis_index("yz")
    core, zz, yh = gx % nc, (gx // nc) % nz, gx // (nc * nz)
    xx, yl = yz % nx, yz // nx
    ny = nyh * nyl
    yy = yh * nyl + yl
    planes, rows, lanes = E.shape
    tiles = rows // 8
    f32 = jnp.float32

    def wrap(a, n):
        return jnp.where(a >= n, a - n, a)

    xn = (jnp.where(gx > 0, gx, ngx) - 1, wrap(gx + 1, ngx))
    yn = (jnp.where(yz > 0, yz, nyz) - 1, wrap(yz + 1, nyz))
    near = [(xn[k], yz) for k in range(2)] + [(gx, yn[k]) for k in range(2)]
    near += [(xn[a], yn[b]) for a in range(2) for b in range(2)]

    def place(y, z, c, x):
        return (((y // nyl) * nz + z) * nc + c, (y % nyl) * nx + x)

    def y_rank(y):
        return jnp.where(y == 0, 0, jnp.where(2 * y <= ny, 2 * y - 1, 2 * (ny - y)))

    def y_of(r):
        return jnp.where(r % 2 == 1, (r + 1) // 2, wrap(ny - r // 2, ny))

    plane = (ny * nx, y_rank(yy) * nx + xx, lambda r: place(y_of(r // nx), zz, core, r % nx))
    column = (nz * nc, zz * nc + core, lambda r: place(yy, r // nc, r % nc, xx))
    groups = (column, plane)
    plane_peers = [place(wrap(yy + a, ny), zz, core, wrap(xx + b, nx)) for a in range(ny) for b in range(nx) if a or b]
    column_peers = [place(yy, wrap(zz + a, nz), wrap(core + b, nc), xx) for a in range(nz) for b in range(nc) if a or b]
    stages = ((column_peers, g0), (plane_peers, g1))

    def each(start, stop, act):
        lax.fori_loop(start, stop, lambda i, c: (act(i), c)[1], 0)

    barrier = pltpu.get_barrier_semaphore()
    for peer in near:
        pl.semaphore_signal(barrier, inc=1, device_id=peer, device_id_type=MESH)
    count = len(near)
    loads = [pltpu.make_async_copy(s, d, in_sem.at[i])
             for i, (s, d) in enumerate(((e_hbm, E), (p_hbm, PT), (m_hbm, M), (b_hbm, B)))]
    for c in loads:
        c.start()
    for size, rank, peer in groups:
        each(rank + 1, size, lambda r: pl.semaphore_signal(barrier, inc=1, device_id=peer(r), device_id_type=MESH))
        count = count + rank

    okx = (gx > 0, gx < ngx - 1)
    oky = (yz > 0, yz < nyz - 1)
    lane = lax.broadcasted_iota(jnp.int32, (8, lanes), 1)
    sub = lax.broadcasted_iota(jnp.int32, (8, lanes), 0)
    ends, seconds = (0, planes - 1), (1, planes - 2)
    rends, rseconds = (0, rows - 1), (1, rows - 2)

    def at(j):
        return slice(8 * j, 8 * j + 8)

    def below(j):
        return slice(8 * j + 1, 8 * j + 9)

    def before(ref, p, j):
        if j == 0:
            return pltpu.roll(ref[p, at(0), :], 1, 0)
        return ref[p, 8 * j - 1:8 * j + 7, :]

    def after(ref, p, j):
        if j == tiles - 1:
            return pltpu.roll(ref[p, at(j), :], 7, 0)
        return ref[p, below(j), :]

    def right_face(e):
        return jnp.where(lane == lanes - 1, 0.0, face(e, pltpu.roll(e, lanes - 1, 1)))

    def along_z(c, v):
        return c * pltpu.roll(v, lanes - 1, 1) + pltpu.roll(c * v, 1, 1)

    EX[...] = jnp.ones(EX.shape, f32)
    CY[:, rows:rows + 8, :] = jnp.zeros((planes, 8, lanes), f32)
    CYH[:, rows:rows + 8, :] = jnp.zeros((2, 8, lanes), f32)

    loads[0].wait()
    for p in range(planes):
        for j in range(tiles):
            e = E[p, at(j), :]
            CZ[p, at(j), :] = right_face(e)
            cy = face(e, before(E, p, j))
            CY[p, at(j), :] = jnp.where(sub == 0, 0.0, cy) if j == 0 else cy
            if p < planes - 1:
                CX[p, at(j), :] = face(e, E[p + 1, at(j), :])
    loads[1].wait()
    loads[2].wait()
    for p in range(planes):
        for j in range(tiles):
            e, cz = E[p, at(j), :], CZ[p, at(j), :]
            pt = PT[p, at(j), :]
            d = 0.25 * M[p, at(j), :].astype(f32) * (jnp.exp(pt) + jnp.exp(-pt))
            d = d + cz + pltpu.roll(cz, 1, 1) + jnp.where((lane == 0) | (lane == lanes - 1), e, 0.0)
            d = d + CY[p, at(j), :] + CY[p, below(j), :]
            if p > 0:
                d = d + CX[p - 1, at(j), :]
            if p < planes - 1:
                d = d + CX[p, at(j), :]
            D0[p, at(j), :] = d
    loads[3].wait()
    for k in range(2):
        for j in range(tiles):
            TS[k, at(j), :] = (CX[0 if k == 0 else planes - 2, at(j), :] * B[seconds[k], at(j), :]
                               / D0[seconds[k], at(j), :])
        for n, ref in enumerate((E, B, D0)):
            for m in range(2):
                RS[k, 2 * n + m:2 * n + m + 1, :] = ref[seconds[k], rends[m]:rends[m] + 1, :]
                GS[k, m, n:n + 1, :] = ref[ends[k], rends[m]:rends[m] + 1, :]
            YS[k, n] = ref[:, rends[k], :]
            YS[k, 3 + n] = ref[:, rseconds[k], :]
        for m in range(2):
            GS[k, m, 3:4, :] = E[seconds[k], rends[m]:rends[m] + 1, :]
            GS[k, m, 4:5, :] = E[ends[k], rseconds[m]:rseconds[m] + 1, :]

    pl.semaphore_wait(barrier, count)
    plan = []
    for n, ref in enumerate((E, B, D0, TS)):
        for k in range(2):
            src = ref.at[k] if n == 3 else ref.at[ends[k]]
            plan.append((src, XB.at[1 - k, n], (xn[k], yz)))
    for k in range(2):
        plan.append((YS.at[k], YB.at[1 - k], (gx, yn[k])))
        plan.append((RS.at[k], RB.at[1 - k], (xn[k], yz)))
        for m in range(2):
            plan.append((GS.at[k, m], GB.at[1 - k, 1 - m], (xn[k], yn[m])))
    sent = []
    for n, (src, dst, dev) in enumerate(plan):
        c = pltpu.make_async_remote_copy(src_ref=src, dst_ref=dst, send_sem=hs_sem.at[n], recv_sem=hr_sem.at[n],
                                         device_id=dev, device_id_type=MESH)
        c.start()
        sent.append(c)
    for n, (size, rank, peer) in enumerate(groups):
        each(0, rank, lambda r: pl.semaphore_signal(here.at[n], inc=1, device_id=peer(r), device_id_type=MESH))
    for c in sent:
        c.wait_recv()

    last = planes + 1
    for m in range(2):
        for n, (row, corner) in enumerate(((0, 0), (1, 1), (2, 2), (3, 4), (4, None), (5, None))):
            EX[m, n, 1:last, :] = YB[m, row]
            if corner is not None:
                EX[m, n, 0:1, :] = GB[0, m, corner:corner + 1, :]
                EX[m, n, last:last + 1, :] = GB[1, m, corner:corner + 1, :]
        EX[m, 6, 0:1, :] = XB[0, 0, rends[m]:rends[m] + 1, :]
        EX[m, 6, 1:last, :] = E[:, rends[m], :]
        EX[m, 6, last:last + 1, :] = XB[1, 0, rends[m]:rends[m] + 1, :]
        e1, b1, p1, e2, b2, p2, e0 = (EX[m, n] for n in range(7))

        def crossing(e, outer):
            lo = face(e, pltpu.roll(e, 1, 0))
            hi = pltpu.roll(lo, 7, 0)
            a_lo, a_hi = jnp.where(okx[0], lo, e), jnp.where(okx[1], hi, e)
            add = jnp.where(sub == 1, a_lo, 0.0) + jnp.where(sub == last - 1, a_hi, 0.0)
            if outer:
                add = add + jnp.where(sub == 0, jnp.where(okx[0], hi, e), 0.0)
                add = add + jnp.where(sub == last, jnp.where(okx[1], lo, e), 0.0)
            return lo, add

        lo, add = crossing(e1, True)
        lo = jnp.where(sub == 1, jnp.where(okx[0], lo, 0.0), lo)
        lo = jnp.where(sub == last, jnp.where(okx[1], lo, 0.0), lo)
        fy = face(e1, e0)
        cy = jnp.where(oky[m], fy, 0.0)
        r1 = 1.0 / (p1 + add + jnp.where(oky[m], fy, e1))
        z1 = b1 * r1
        t = face(e1, e2) * b2 / (p2 + crossing(e2, False)[1])
        t = t + along_z(right_face(e1), z1)
        t = t + lo * pltpu.roll(z1, 1, 0) + pltpu.roll(lo, 7, 0) * pltpu.roll(z1, 7, 0)
        ADD[m] = jnp.where(oky[m], fy, e0)
        CY1[m], Z1[m], R1[m], N1[m], PZ[m] = cy, z1, r1, t, cy * z1
        for k in range(2):
            T2[k, 0, m:m + 1, :] = XB[k, 0, rends[m]:rends[m] + 1, :]
            T2[k, 1, m:m + 1, :] = GB[k, m, 3:4, :]
    for k in range(2):
        e1, ed = T2[k, 0], T2[k, 1]
        e2, b2, d2 = RB[k, 0:2, :], RB[k, 2:4, :], RB[k, 4:6, :]
        f = face(e2, ed)
        row2 = lax.broadcasted_iota(jnp.int32, (2, lanes), 0)
        f = jnp.where(row2 == 0, jnp.where(oky[0], f, e2), jnp.where(oky[1], f, e2))
        T4[k] = face(e1, e2) * b2 / (d2 + f)

    def end_rows(j, p1, ref, k0=0):
        t = 0.0
        if j == 0:
            t = t + jnp.where(sub == 0, ref[0, p1:p1 + 1, :], 0.0)
        if j == tiles - 1:
            t = t + jnp.where(sub == 7, ref[1, p1:p1 + 1, :], 0.0)
        return t

    for k, p in enumerate(ends):
        h = last * k
        for j in range(tiles):
            e, eh = E[p, at(j), :], XB[k, 0, at(j), :]
            fx = face(e, eh)
            CXE[k, at(j), :] = jnp.where(okx[k], fx, 0.0)
            d = D0[p, at(j), :] + jnp.where(okx[k], fx, e)
            dh = XB[k, 2, at(j), :] + jnp.where(okx[k], fx, eh)
            if j in (0, tiles - 1):
                d = d + end_rows(j, p + 1, ADD)
                dh = dh + end_rows(j, h, ADD)
            rd, rh = 1.0 / d, 1.0 / dh
            D[p, at(j), :] = d
            RD[p, at(j), :] = rd
            Z[p, at(j), :] = B[p, at(j), :] * rd
            RH[k, at(j), :] = rh
            ZH[k, at(j), :] = XB[k, 1, at(j), :] * rh
            CZH[k, at(j), :] = right_face(eh)
            cy = face(eh, before(XB.at[k], 0, j))
            CYH[k, at(j), :] = jnp.where(sub == 0, 0.0, cy) if j == 0 else cy
    for p in range(1, planes - 1):
        for j in range(tiles):
            d = D0[p, at(j), :]
            if j in (0, tiles - 1):
                d = d + end_rows(j, p + 1, ADD)
            rd = 1.0 / d
            D[p, at(j), :] = d
            RD[p, at(j), :] = rd
            Z[p, at(j), :] = B[p, at(j), :] * rd

    def image(V, VH, PV, p, j):
        v = V[p, at(j), :]
        t = D[p, at(j), :] * v - along_z(CZ[p, at(j), :], v)
        t = t - CY[p, at(j), :] * before(V, p, j) - CY[p, below(j), :] * after(V, p, j)
        if p > 0:
            t = t - CX[p - 1, at(j), :] * V[p - 1, at(j), :]
        else:
            t = t - CXE[0, at(j), :] * VH[0, at(j), :]
        if p < planes - 1:
            t = t - CX[p, at(j), :] * V[p + 1, at(j), :]
        else:
            t = t - CXE[1, at(j), :] * VH[1, at(j), :]
        if j in (0, tiles - 1):
            t = t - end_rows(j, p + 1, PV)
        return t

    s0 = s1 = s2 = s3 = jnp.zeros((8, lanes), f32)
    for p in range(planes):
        for j in range(tiles):
            z = Z[p, at(j), :]
            q = image(Z, ZH, PZ, p, j)
            u = q * RD[p, at(j), :]
            Q[p, at(j), :] = q
            U[p, at(j), :] = u
            s0 = s0 + B[p, at(j), :] * z
            s1 = s1 + z * q
            s2 = s2 + q * u
    for m in range(2):
        EX[m, 7, 1:last, :] = Z[:, rends[m], :]
        t = N1[m] + CY1[m] * EX[m, 7]
        PU[m] = CY1[m] * (Z1[m] - t * R1[m])
    for k, p in enumerate(ends):
        h = last * k
        for j in range(tiles):
            v = ZH[k, at(j), :]
            t = XB[k, 3, at(j), :]
            if j == 0:
                t = jnp.where(sub == 0, T4[k, 0:1, :], t)
            if j == tiles - 1:
                t = jnp.where(sub == 7, T4[k, 1:2, :], t)
            t = t + CXE[k, at(j), :] * Z[p, at(j), :] + along_z(CZH[k, at(j), :], v)
            t = t + CYH[k, at(j), :] * before(ZH, k, j) + CYH[k, below(j), :] * after(ZH, k, j)
            if j in (0, tiles - 1):
                t = t + end_rows(j, h, PZ)
            UH[k, at(j), :] = v - t * RH[k, at(j), :]
    for p in range(planes):
        for j in range(tiles):
            w = image(U, UH, PU, p, j)
            W[p, at(j), :] = w
            s3 = s3 + U[p, at(j), :] * w

    def folded(s):
        t = s[:, :128]
        for i in range(128, lanes, 128):
            t = t + s[:, i:i + 128]
        return jnp.sum(t, axis=0, keepdims=True)

    lane1 = lax.broadcasted_iota(jnp.int32, (1, 128), 1)
    message = jnp.zeros((1, 128), f32)
    for k, t in enumerate((s0, s1, s2, s3)):
        t = folded(t)
        t = t + pltpu.roll(t, 64, 1)
        t = t + pltpu.roll(t, 32, 1)
        message = jnp.where(lane1 // 32 == k, t, message)
    part[0] = message
    for n, ((peers, got), (size, rank, peer)) in enumerate(zip(stages, groups)):
        @pl.when(rank < size - 1)
        def _():
            pl.semaphore_wait(here.at[n], size - 1 - rank)

        for d, dev in enumerate(peers):
            pltpu.make_async_remote_copy(src_ref=part.at[n], dst_ref=got.at[d], send_sem=as_sem.at[n],
                                         recv_sem=ar_sem.at[n], device_id=dev, device_id_type=MESH).start()
        total = part[n]
        if peers:
            pltpu.make_async_copy(got, got, ar_sem.at[n]).wait()
            for d in range(len(peers)):
                total = total + got[d]
        part[n + 1] = total
    row4 = lax.broadcasted_iota(jnp.int32, (4, 128), 0)
    lane4 = lax.broadcasted_iota(jnp.int32, (4, 128), 1)
    s = jnp.sum(jnp.where(lane4 // 32 == row4, part[2], 0.0), axis=1, keepdims=True)
    s0, s1, s2, s3 = s[0:1], s[1:2], s[2:3], s[3:4]
    a, g, h = s0 / s1, s2 / s1, s3 / s1
    cu = (a * g - 1.0) / (h - g * g)
    cz = a + g * cu
    coef[0:1, :] = jnp.broadcast_to(cz, (1, 128))
    coef[1:2, :] = jnp.broadcast_to(cu, (1, 128))
    for n, (peers, got) in enumerate(stages):
        if peers:
            pltpu.make_async_copy(got, got, as_sem.at[n]).wait()
    for d in sent:
        d.wait_send()


def local(sizes, right_side, potential, permittivity, ion_mask):
    f32 = jnp.float32
    planes, rows, lanes = block = right_side.shape
    columns, in_plane = sizes["z"] * sizes["core"], sizes["x"] * sizes["y_hi"] * sizes["y_lo"]
    vm = lambda *s: pltpu.VMEM(s, f32)
    full, pad = vm(*block), vm(2, 8, lanes)
    side = vm(2, rows, lanes)
    scratch = [
        full, full, pltpu.VMEM(block, jnp.int32),
        vm(planes - 1, rows, lanes), side, vm(planes, rows + 8, lanes), full, full, full, full, side,
        vm(2, 4, rows, lanes), vm(2, 8, lanes), vm(2, 6, planes, lanes), vm(2, 2, 8, lanes),
        vm(2, 8, lanes), vm(2, 6, planes, lanes), vm(2, 2, 8, lanes),
        vm(2, 8, 8, lanes), vm(2, 2, 2, lanes), vm(2, 2, lanes),
        vm(2, rows + 8, lanes), side, side, side, side, pad, pad, pad, pad, pad, pad, pad,
        vm(3, 1, 128), vm(max(columns - 1, 1), 1, 128), vm(max(in_plane - 1, 1), 1, 128),
        pltpu.SemaphoreType.DMA((4,)),
        pltpu.SemaphoreType.DMA((16,)), pltpu.SemaphoreType.DMA((16,)),
        pltpu.SemaphoreType.DMA((2,)), pltpu.SemaphoreType.DMA((2,)), pltpu.SemaphoreType.REGULAR((2,)),
    ]
    hbm, vmem = pl.BlockSpec(memory_space=pltpu.HBM), pl.BlockSpec(memory_space=pltpu.VMEM)
    args = (right_side, potential, permittivity, ion_mask)
    whole = jax.ShapeDtypeStruct(block, f32)
    fields = pl.pallas_call(
        functools.partial(kernel, sizes),
        out_shape=(whole,) * 5 + (jax.ShapeDtypeStruct((2, 128), f32),),
        in_specs=[hbm] * 4,
        out_specs=(vmem,) * 6,
        scratch_shapes=scratch,
        compiler_params=pltpu.CompilerParams(collective_id=0, has_side_effects=True, vmem_limit_bytes=24 * 2**20),
    )(*[pltpu.with_memory_space_constraint(a, pltpu.HBM) for a in args])
    return pl.pallas_call(
        finish,
        out_shape=(whole, whole),
        in_specs=[vmem] * 6,
        out_specs=(hbm, hbm),
        scratch_shapes=[full, full, pltpu.SemaphoreType.DMA((2, planes))],
        compiler_params=pltpu.CompilerParams(vmem_limit_bytes=16 * 2**20),
    )(*fields)


def finish(B, Z, U, Q, W, coef, x_out, r_out, X, R, sem):
    cz, cu = coef[0:1, 0:1], coef[1:2, 0:1]
    stores = []
    for p in range(B.shape[0]):
        X[p] = cz * Z[p] - cu * U[p]
        R[p] = B[p] - cz * Q[p] + cu * W[p]
        for i, (src, dst) in enumerate(((X, x_out), (R, r_out))):
            c = pltpu.make_async_copy(src.at[p], dst.at[p], sem.at[i, p])
            c.start()
            stores.append(c)
    for c in stores:
        c.wait()


def solution(mesh, sizes=SIZES):
    spec = P("gx", "yz", None)
    return jax.shard_map(functools.partial(local, sizes), mesh=mesh, in_specs=(spec,) * 4, out_specs=(spec,) * 2,
                         check_vma=False)
```

```python
import functools

import jax
import jax.numpy as jnp
from jax import lax
from jax.experimental import pallas as pl
from jax.experimental.pallas import tpu as pltpu
from jax.sharding import PartitionSpec as P

MESH = pl.DeviceIdType.MESH
SIZES = dict(y_hi=4, z=12, core=2, y_lo=2, x=4)


def face(a, b):
    return (2.0 * a * b) / (a + b)


def div(a, n):
    return a >> (n.bit_length() - 1) if n & (n - 1) == 0 else lax.div(a, jnp.int32(n))


def mod(a, n):
    return a & (n - 1) if n & (n - 1) == 0 else a - div(a, n) * n


def kernel(sizes, b_hbm, p_hbm, e_hbm, m_hbm, B, Z, U, Q, W, coef,
           PT, E, M, CX, CXE, CY, CZ, D0, D, RD, TS,
           XB, RB, YB, RS, YS, EX, T2, T4, CYH, CZH, ZH, RH, UH, ADD, CY1, Z1, R1, N1, PZ, PU,
           part, g0, g1, in_sem, hs_sem, hr_sem, as_sem, ar_sem, here, close):
    nyh, nz, nc, nyl, nx = (sizes[k] for k in ("y_hi", "z", "core", "y_lo", "x"))
    ngx, nyz = nyh * nz * nc, nyl * nx
    gx, yz = lax.axis_index("gx"), lax.axis_index("yz")
    core, yh = mod(gx, nc), div(gx, nz * nc)
    zz = div(gx - yh * (nz * nc), nc)
    xx, yl = mod(yz, nx), div(yz, nx)
    ny = nyh * nyl
    yy = yh * nyl + yl
    planes, rows, lanes = E.shape
    tiles = rows // 8
    f32 = jnp.float32

    def wrap(a, n):
        return jnp.where(a >= n, a - n, a)

    xn = (jnp.where(gx > 0, gx, ngx) - 1, wrap(gx + 1, ngx))
    yn = (jnp.where(yz > 0, yz, nyz) - 1, wrap(yz + 1, nyz))
    near = [(xn[k], yz) for k in range(2)] + [(gx, yn[k]) for k in range(2)]

    def place(y, z, c, x):
        return ((div(y, nyl) * nz + z) * nc + c, mod(y, nyl) * nx + x)

    def y_rank(y):
        return jnp.where(y == 0, 0, jnp.where(2 * y <= ny, 2 * y - 1, 2 * (ny - y)))

    column_rank, my_y = zz * nc + core, y_rank(yy)
    my_plane = my_y * nx + xx
    y_order = sorted(range(ny), key=lambda y: min(y, ny - y) * 2 + (2 * y > ny))
    sizes_ranks = ((nz * nc, column_rank), (ny * nx, my_plane))

    def far(a, n):
        return min(a, n - a)

    offsets = sorted(((a, b) for a in range(ny) for b in range(nx) if a or b), key=lambda o: -far(o[0], ny) - far(o[1], nx))
    plane_peers = [place(wrap(yy + a, ny), zz, core, wrap(xx + b, nx)) for a, b in offsets]
    column_peers = [place(yy, wrap(zz + a, nz), wrap(core + b, nc), xx) for a in range(nz) for b in range(nc) if a or b]
    stages = ((column_peers, g0), (plane_peers, g1))

    def signal(sem, dev):
        pl.semaphore_signal(sem, inc=1, device_id=dev, device_id_type=MESH)

    def each(start, stop, act):
        lax.fori_loop(start, stop, lambda i, c: (act(i), c)[1], 0)

    def group_signals(sems, later):
        base = gx - column_rank
        if later:
            each(column_rank + 1, nz * nc, lambda r: signal(sems[0], (base + r, yz)))
        else:
            each(0, column_rank, lambda r: signal(sems[0], (base + r, yz)))
        for r, y in enumerate(y_order):
            g, q = (y // nyl) * nz * nc + column_rank, (y % nyl) * nx

            @pl.when(r > my_y if later else r < my_y)
            def _():
                for x in range(nx):
                    signal(sems[1], (g, q + x))

        if later:
            each(xx + 1, nx, lambda x: signal(sems[1], (gx, yl * nx + x)))
        else:
            each(0, xx, lambda x: signal(sems[1], (gx, yl * nx + x)))

    okx = (gx > 0, gx < ngx - 1)
    oky = (yz > 0, yz < nyz - 1)
    earlier = [column_rank > 0, column_rank == nz * nc - 1]
    earlier += [y_rank(yh * nyl + div(q, nx)) * nx + mod(q, nx) < my_plane for q in yn]
    mirror = (1, 0, 3, 2)
    ok = okx + oky
    later = [jnp.logical_and(ok[n], jnp.logical_not(earlier[n])) for n in range(4)]
    earlier = [jnp.logical_and(ok[n], earlier[n]) for n in range(4)]
    loads = [pltpu.make_async_copy(s, d, in_sem.at[i])
             for i, (s, d) in enumerate(((e_hbm, E), (p_hbm, PT), (m_hbm, M), (b_hbm, B)))]
    for c in loads:
        c.start()
    barrier = pltpu.get_barrier_semaphore()
    count = column_rank + my_plane
    for n, dev in enumerate(near):
        pl.when(later[n])(functools.partial(signal, barrier, dev))
        count = count + jnp.where(earlier[n], 1, 0)
    group_signals((barrier, barrier), True)

    lane = lax.broadcasted_iota(jnp.int32, (8, lanes), 1)
    sub = lax.broadcasted_iota(jnp.int32, (8, lanes), 0)
    ends, seconds = (0, planes - 1), (1, planes - 2)
    rends, rseconds = (0, rows - 1), (1, rows - 2)

    def at(j):
        return slice(8 * j, 8 * j + 8)

    def below(j):
        return slice(8 * j + 1, 8 * j + 9)

    def before(ref, p, j):
        if j == 0:
            return pltpu.roll(ref[p, at(0), :], 1, 0)
        return ref[p, 8 * j - 1:8 * j + 7, :]

    def after(ref, p, j):
        if j == tiles - 1:
            return pltpu.roll(ref[p, at(j), :], 7, 0)
        return ref[p, below(j), :]

    def right_face(e):
        return jnp.where(lane == lanes - 1, 0.0, face(e, pltpu.roll(e, lanes - 1, 1)))

    def along_z(c, v):
        return c * pltpu.roll(v, lanes - 1, 1) + pltpu.roll(c * v, 1, 1)

    for n in range(4):
        @pl.when(jnp.logical_not(ok[n]))
        def _():
            for ref in ((XB, RB) if n < 2 else (YB,)):
                ref[n % 2] = jnp.ones(ref.shape[1:], f32)

    EX[...] = jnp.ones(EX.shape, f32)
    CY[:, rows:rows + 8, :] = jnp.zeros((planes, 8, lanes), f32)
    CYH[:, rows:rows + 8, :] = jnp.zeros((2, 8, lanes), f32)

    @pl.when(count > 0)
    def _():
        pl.semaphore_wait(barrier, count)

    for n, dev in enumerate(near):
        pl.when(earlier[n])(functools.partial(signal, close.at[mirror[n]], dev))

    loads[0].wait()
    for p in range(planes):
        for j in range(tiles):
            e = E[p, at(j), :]
            CZ[p, at(j), :] = right_face(e)
            cy = face(e, before(E, p, j))
            CY[p, at(j), :] = jnp.where(sub == 0, 0.0, cy) if j == 0 else cy
            if p < planes - 1:
                CX[p, at(j), :] = face(e, E[p + 1, at(j), :])
    loads[1].wait()
    loads[2].wait()
    for p in range(planes):
        for j in range(tiles):
            e, cz = E[p, at(j), :], CZ[p, at(j), :]
            pt = PT[p, at(j), :]
            d = 0.25 * M[p, at(j), :].astype(f32) * (jnp.exp(pt) + jnp.exp(-pt))
            d = d + cz + pltpu.roll(cz, 1, 1) + jnp.where((lane == 0) | (lane == lanes - 1), e, 0.0)
            d = d + CY[p, at(j), :] + CY[p, below(j), :]
            if p > 0:
                d = d + CX[p - 1, at(j), :]
            if p < planes - 1:
                d = d + CX[p, at(j), :]
            D0[p, at(j), :] = d
    loads[3].wait()
    for k in range(2):
        for j in range(tiles):
            TS[k, at(j), :] = (CX[0 if k == 0 else planes - 2, at(j), :] * B[seconds[k], at(j), :]
                               / D0[seconds[k], at(j), :])
        for n, ref in enumerate((E, B, D0)):
            for m in range(2):
                RS[k, 2 * n + m:2 * n + m + 1, :] = ref[seconds[k], rends[m]:rends[m] + 1, :]
            YS[k, n] = ref[:, rends[k], :]
            YS[k, 3 + n] = ref[:, rseconds[k], :]

    plan = [[] for _ in near]
    for k in range(2):
        plan[2 + k].append((YS.at[k], YB.at[1 - k]))
        for n, ref in enumerate((E, B, D0, TS)):
            plan[k].append((ref.at[k] if n == 3 else ref.at[ends[k]], XB.at[1 - k, n]))
        plan[k].append((RS.at[k], RB.at[1 - k]))
    total, sent = 0, [[] for _ in near]
    for n, dev in enumerate(near):
        for src, dst in plan[n]:
            sent[n].append(pltpu.make_async_remote_copy(
                src_ref=src, dst_ref=dst, send_sem=hs_sem.at[total], recv_sem=hr_sem.at[total],
                device_id=dev, device_id_type=MESH))
            total += 1
    order = (2, 3, 1, 0)

    def send(n):
        for c in sent[n][:4]:
            c.start()

    def send_later(n):
        pl.semaphore_wait(close.at[n], 1)
        send(n)

    for n in order:
        pl.when(earlier[n])(functools.partial(send, n))
    group_signals((here.at[0], here.at[1]), False)
    for n in order[:3]:
        pl.when(later[n])(functools.partial(send_later, n))

    for n in (2, 3):
        pl.when(ok[mirror[n]])(sent[n][0].wait_recv)
    for k in range(2):
        for m in range(2):
            for n, (row, p) in enumerate(((0, ends[k]), (1, ends[k]), (2, ends[k]), (0, seconds[k]), (3, ends[k]))):
                RS[k, 6 + 5 * m + n:7 + 5 * m + n, :] = YB[m, row, p:p + 1, :]
    pl.when(ok[1])(sent[1][4].start)

    @pl.when(later[0])
    def _():
        pl.semaphore_wait(close.at[0], 1)

    pl.when(ok[0])(sent[0][4].start)
    pl.when(later[0])(functools.partial(send, 0))
    for n in (1, 0):
        @pl.when(ok[mirror[n]])
        def _():
            for c in (*sent[n][:3], sent[n][4]):
                c.wait_recv()

    last = planes + 1
    for m in range(2):
        for n, (row, corner) in enumerate(((0, 0), (1, 1), (2, 2), (3, 4), (4, None), (5, None))):
            EX[m, n, 1:last, :] = YB[m, row]
            if corner is not None:
                EX[m, n, 0:1, :] = RB[0, 6 + 5 * m + corner:7 + 5 * m + corner, :]
                EX[m, n, last:last + 1, :] = RB[1, 6 + 5 * m + corner:7 + 5 * m + corner, :]
        EX[m, 6, 0:1, :] = XB[0, 0, rends[m]:rends[m] + 1, :]
        EX[m, 6, 1:last, :] = E[:, rends[m], :]
        EX[m, 6, last:last + 1, :] = XB[1, 0, rends[m]:rends[m] + 1, :]
        e1, b1, p1, e2, b2, p2, e0 = (EX[m, n] for n in range(7))

        def crossing(e, outer):
            lo = face(e, pltpu.roll(e, 1, 0))
            hi = pltpu.roll(lo, 7, 0)
            a_lo, a_hi = jnp.where(okx[0], lo, e), jnp.where(okx[1], hi, e)
            add = jnp.where(sub == 1, a_lo, 0.0) + jnp.where(sub == last - 1, a_hi, 0.0)
            if outer:
                add = add + jnp.where(sub == 0, jnp.where(okx[0], hi, e), 0.0)
                add = add + jnp.where(sub == last, jnp.where(okx[1], lo, e), 0.0)
            return lo, add

        lo, add = crossing(e1, True)
        lo = jnp.where(sub == 1, jnp.where(okx[0], lo, 0.0), lo)
        lo = jnp.where(sub == last, jnp.where(okx[1], lo, 0.0), lo)
        fy = face(e1, e0)
        cy = jnp.where(oky[m], fy, 0.0)
        r1 = 1.0 / (p1 + add + jnp.where(oky[m], fy, e1))
        z1 = b1 * r1
        t = face(e1, e2) * b2 / (p2 + crossing(e2, False)[1])
        t = t + along_z(right_face(e1), z1)
        t = t + lo * pltpu.roll(z1, 1, 0) + pltpu.roll(lo, 7, 0) * pltpu.roll(z1, 7, 0)
        ADD[m] = jnp.where(oky[m], fy, e0)
        CY1[m], Z1[m], R1[m], N1[m], PZ[m] = cy, z1, r1, t, cy * z1
        for k in range(2):
            T2[k, 0, m:m + 1, :] = XB[k, 0, rends[m]:rends[m] + 1, :]
            T2[k, 1, m:m + 1, :] = RB[k, 9 + 5 * m:10 + 5 * m, :]
    for k in range(2):
        e1, ed = T2[k, 0], T2[k, 1]
        e2, b2, d2 = RB[k, 0:2, :], RB[k, 2:4, :], RB[k, 4:6, :]
        f = face(e2, ed)
        row2 = lax.broadcasted_iota(jnp.int32, (2, lanes), 0)
        f = jnp.where(row2 == 0, jnp.where(oky[0], f, e2), jnp.where(oky[1], f, e2))
        T4[k] = face(e1, e2) * b2 / (d2 + f)

    def end_rows(j, p1, ref, k0=0):
        t = 0.0
        if j == 0:
            t = t + jnp.where(sub == 0, ref[0, p1:p1 + 1, :], 0.0)
        if j == tiles - 1:
            t = t + jnp.where(sub == 7, ref[1, p1:p1 + 1, :], 0.0)
        return t

    for k, p in enumerate(ends):
        h = last * k
        for j in range(tiles):
            e, eh = E[p, at(j), :], XB[k, 0, at(j), :]
            fx = face(e, eh)
            CXE[k, at(j), :] = jnp.where(okx[k], fx, 0.0)
            d = D0[p, at(j), :] + jnp.where(okx[k], fx, e)
            dh = XB[k, 2, at(j), :] + jnp.where(okx[k], fx, eh)
            if j in (0, tiles - 1):
                d = d + end_rows(j, p + 1, ADD)
                dh = dh + end_rows(j, h, ADD)
            rd, rh = 1.0 / d, 1.0 / dh
            D[p, at(j), :] = d
            RD[p, at(j), :] = rd
            Z[p, at(j), :] = B[p, at(j), :] * rd
            RH[k, at(j), :] = rh
            ZH[k, at(j), :] = XB[k, 1, at(j), :] * rh
            CZH[k, at(j), :] = right_face(eh)
            cy = face(eh, before(XB.at[k], 0, j))
            CYH[k, at(j), :] = jnp.where(sub == 0, 0.0, cy) if j == 0 else cy
    for p in range(1, planes - 1):
        for j in range(tiles):
            d = D0[p, at(j), :]
            if j in (0, tiles - 1):
                d = d + end_rows(j, p + 1, ADD)
            rd = 1.0 / d
            D[p, at(j), :] = d
            RD[p, at(j), :] = rd
            Z[p, at(j), :] = B[p, at(j), :] * rd

    def image(V, VH, PV, p, j):
        v = V[p, at(j), :]
        t = D[p, at(j), :] * v - along_z(CZ[p, at(j), :], v)
        t = t - CY[p, at(j), :] * before(V, p, j) - CY[p, below(j), :] * after(V, p, j)
        if p > 0:
            t = t - CX[p - 1, at(j), :] * V[p - 1, at(j), :]
        else:
            t = t - CXE[0, at(j), :] * VH[0, at(j), :]
        if p < planes - 1:
            t = t - CX[p, at(j), :] * V[p + 1, at(j), :]
        else:
            t = t - CXE[1, at(j), :] * VH[1, at(j), :]
        if j in (0, tiles - 1):
            t = t - end_rows(j, p + 1, PV)
        return t

    s0 = s1 = s2 = s3 = jnp.zeros((8, lanes), f32)
    for p in range(planes):
        for j in range(tiles):
            z = Z[p, at(j), :]
            q = image(Z, ZH, PZ, p, j)
            u = q * RD[p, at(j), :]
            Q[p, at(j), :] = q
            U[p, at(j), :] = u
            s0 = s0 + B[p, at(j), :] * z
            s1 = s1 + z * q
            s2 = s2 + q * u
    for m in range(2):
        EX[m, 7, 1:last, :] = Z[:, rends[m], :]
        t = N1[m] + CY1[m] * EX[m, 7]
        PU[m] = CY1[m] * (Z1[m] - t * R1[m])
    for n in range(2):
        pl.when(ok[mirror[n]])(sent[n][3].wait_recv)
    for k, p in enumerate(ends):
        h = last * k
        for j in range(tiles):
            v = ZH[k, at(j), :]
            t = XB[k, 3, at(j), :]
            if j == 0:
                t = jnp.where(sub == 0, T4[k, 0:1, :], t)
            if j == tiles - 1:
                t = jnp.where(sub == 7, T4[k, 1:2, :], t)
            t = t + CXE[k, at(j), :] * Z[p, at(j), :] + along_z(CZH[k, at(j), :], v)
            t = t + CYH[k, at(j), :] * before(ZH, k, j) + CYH[k, below(j), :] * after(ZH, k, j)
            if j in (0, tiles - 1):
                t = t + end_rows(j, h, PZ)
            UH[k, at(j), :] = v - t * RH[k, at(j), :]
    for p in range(planes):
        for j in range(tiles):
            w = image(U, UH, PU, p, j)
            W[p, at(j), :] = w
            s3 = s3 + U[p, at(j), :] * w

    def folded(s):
        t = s[:, :128]
        for i in range(128, lanes, 128):
            t = t + s[:, i:i + 128]
        return jnp.sum(t, axis=0, keepdims=True)

    lane1 = lax.broadcasted_iota(jnp.int32, (1, 128), 1)
    message = jnp.zeros((1, 128), f32)
    for k, t in enumerate((s0, s1, s2, s3)):
        t = folded(t)
        t = t + pltpu.roll(t, 64, 1)
        t = t + pltpu.roll(t, 32, 1)
        message = jnp.where(lane1 // 32 == k, t, message)
    part[0] = message
    for n, ((peers, got), (size, rank)) in enumerate(zip(stages, sizes_ranks)):
        @pl.when(rank < size - 1)
        def _():
            pl.semaphore_wait(here.at[n], size - 1 - rank)

        for d, dev in enumerate(peers):
            pltpu.make_async_remote_copy(src_ref=part.at[n], dst_ref=got.at[d], send_sem=as_sem.at[n],
                                         recv_sem=ar_sem.at[n], device_id=dev, device_id_type=MESH).start()
        total = part[n]
        if peers:
            pltpu.make_async_copy(got, got, ar_sem.at[n]).wait()
            for d in range(len(peers)):
                total = total + got[d]
        part[n + 1] = total
    row4 = lax.broadcasted_iota(jnp.int32, (4, 128), 0)
    lane4 = lax.broadcasted_iota(jnp.int32, (4, 128), 1)
    s = jnp.sum(jnp.where(lane4 // 32 == row4, part[2], 0.0), axis=1, keepdims=True)
    s0, s1, s2, s3 = s[0:1], s[1:2], s[2:3], s[3:4]
    a, g, h = s0 / s1, s2 / s1, s3 / s1
    cu = (a * g - 1.0) / (h - g * g)
    cz = a + g * cu
    coef[0:1, :] = jnp.broadcast_to(cz, (1, 128))
    coef[1:2, :] = jnp.broadcast_to(cu, (1, 128))
    for n, (peers, got) in enumerate(stages):
        if peers:
            pltpu.make_async_copy(got, got, as_sem.at[n]).wait()
    for n in range(4):
        @pl.when(ok[n])
        def _():
            for c in sent[n]:
                c.wait_send()


def local(sizes, right_side, potential, permittivity, ion_mask):
    f32 = jnp.float32
    planes, rows, lanes = block = right_side.shape
    columns, in_plane = sizes["z"] * sizes["core"], sizes["x"] * sizes["y_hi"] * sizes["y_lo"]
    vm = lambda *s: pltpu.VMEM(s, f32)
    full, pad = vm(*block), vm(2, 8, lanes)
    side = vm(2, rows, lanes)
    scratch = [
        full, full, pltpu.VMEM(block, jnp.int32),
        vm(planes - 1, rows, lanes), side, vm(planes, rows + 8, lanes), full, full, full, full, side,
        vm(2, 4, rows, lanes), vm(2, 16, lanes), vm(2, 6, planes, lanes), vm(2, 16, lanes), vm(2, 6, planes, lanes),
        vm(2, 8, 8, lanes), vm(2, 2, 2, lanes), vm(2, 2, lanes),
        vm(2, rows + 8, lanes), side, side, side, side, pad, pad, pad, pad, pad, pad, pad,
        vm(3, 1, 128), vm(max(columns - 1, 1), 1, 128), vm(max(in_plane - 1, 1), 1, 128),
        pltpu.SemaphoreType.DMA((4,)),
        pltpu.SemaphoreType.DMA((12,)), pltpu.SemaphoreType.DMA((12,)),
        pltpu.SemaphoreType.DMA((2,)), pltpu.SemaphoreType.DMA((2,)), pltpu.SemaphoreType.REGULAR((2,)),
        pltpu.SemaphoreType.REGULAR((4,)),
    ]
    hbm, vmem = pl.BlockSpec(memory_space=pltpu.HBM), pl.BlockSpec(memory_space=pltpu.VMEM)
    args = (right_side, potential, permittivity, ion_mask)
    whole = jax.ShapeDtypeStruct(block, f32)
    fields = pl.pallas_call(
        functools.partial(kernel, sizes),
        out_shape=(whole,) * 5 + (jax.ShapeDtypeStruct((2, 128), f32),),
        in_specs=[hbm] * 4,
        out_specs=(vmem,) * 6,
        scratch_shapes=scratch,
        compiler_params=pltpu.CompilerParams(collective_id=0, has_side_effects=True, vmem_limit_bytes=24 * 2**20),
    )(*[pltpu.with_memory_space_constraint(a, pltpu.HBM) for a in args])
    return pl.pallas_call(
        finish,
        out_shape=(whole, whole),
        in_specs=[vmem] * 6,
        out_specs=(hbm, hbm),
        scratch_shapes=[full, full, pltpu.SemaphoreType.DMA((2, planes))],
        compiler_params=pltpu.CompilerParams(vmem_limit_bytes=16 * 2**20),
    )(*fields)


def finish(B, Z, U, Q, W, coef, x_out, r_out, X, R, sem):
    cz, cu = coef[0:1, 0:1], coef[1:2, 0:1]
    stores = []
    for p in range(B.shape[0]):
        X[p] = cz * Z[p] - cu * U[p]
        R[p] = B[p] - cz * Q[p] + cu * W[p]
        for i, (src, dst) in enumerate(((X, x_out), (R, r_out))):
            c = pltpu.make_async_copy(src.at[p], dst.at[p], sem.at[i, p])
            c.start()
            stores.append(c)
    for c in stores:
        c.wait()


def solution(mesh, sizes=SIZES):
    spec = P("gx", "yz", None)
    return jax.shard_map(functools.partial(local, sizes), mesh=mesh, in_specs=(spec,) * 4, out_specs=(spec,) * 2,
                         check_vma=False)
```

```python
import functools

import jax
import jax.numpy as jnp
from jax import lax
from jax.experimental import pallas as pl
from jax.experimental.pallas import tpu as pltpu
from jax.sharding import PartitionSpec as P

MESH = pl.DeviceIdType.MESH
SIZES = dict(y_hi=4, z=12, core=2, y_lo=2, x=4)


def face(a, b):
    return (2.0 * a * b) / (a + b)


def div(a, n):
    return a >> (n.bit_length() - 1) if n & (n - 1) == 0 else lax.div(a, jnp.int32(n))


def mod(a, n):
    return a & (n - 1) if n & (n - 1) == 0 else a - div(a, n) * n


def kernel(sizes, b_hbm, p_hbm, e_hbm, m_hbm, B, Z, U, Q, W, coef,
           PT, E, M, CX, CXE, CY, CZ, D0, D, RD, TS,
           XB, RB, YB, RS, YS, EX, T2, T4, CYH, CZH, ZH, RH, UH, ADD, CY1, Z1, R1, N1, PZ, PU,
           part, g0, g1, in_sem, hs_sem, hr_sem, as_sem, ar_sem, here, close):
    nyh, nz, nc, nyl, nx = (sizes[k] for k in ("y_hi", "z", "core", "y_lo", "x"))
    ngx, nyz = nyh * nz * nc, nyl * nx
    gx, yz = lax.axis_index("gx"), lax.axis_index("yz")
    core, yh = mod(gx, nc), div(gx, nz * nc)
    zz = div(gx - yh * (nz * nc), nc)
    xx, yl = mod(yz, nx), div(yz, nx)
    ny = nyh * nyl
    yy = yh * nyl + yl
    planes, rows, lanes = E.shape
    tiles = rows // 8
    f32 = jnp.float32

    def wrap(a, n):
        return jnp.where(a >= n, a - n, a)

    xn = (jnp.where(gx > 0, gx, ngx) - 1, wrap(gx + 1, ngx))
    yn = (jnp.where(yz > 0, yz, nyz) - 1, wrap(yz + 1, nyz))
    near = [(xn[k], yz) for k in range(2)] + [(gx, yn[k]) for k in range(2)]

    def place(y, z, c, x):
        return ((div(y, nyl) * nz + z) * nc + c, mod(y, nyl) * nx + x)

    def y_rank(y):
        return jnp.where(y == 0, 0, jnp.where(2 * y <= ny, 2 * y - 1, 2 * (ny - y)))

    column_rank, my_y = zz * nc + core, y_rank(yy)
    my_plane = my_y * nx + xx
    y_order = sorted(range(ny), key=lambda y: min(y, ny - y) * 2 + (2 * y > ny))
    sizes_ranks = ((nz * nc, column_rank), (ny * nx, my_plane))

    def far(a, n):
        return min(a, n - a)

    offsets = sorted(((a, b) for a in range(ny) for b in range(nx) if a or b), key=lambda o: -far(o[0], ny) - far(o[1], nx))
    plane_peers = [place(wrap(yy + a, ny), zz, core, wrap(xx + b, nx)) for a, b in offsets]
    column_peers = [place(yy, wrap(zz + a, nz), wrap(core + b, nc), xx) for a in range(nz) for b in range(nc) if a or b]
    stages = ((column_peers, g0), (plane_peers, g1))

    def signal(sem, dev):
        pl.semaphore_signal(sem, inc=1, device_id=dev, device_id_type=MESH)

    def each(start, stop, act):
        lax.fori_loop(start, stop, lambda i, c: (act(i), c)[1], 0)

    def group_signals(sems, later):
        base = gx - column_rank
        if later:
            each(column_rank + 1, nz * nc, lambda r: signal(sems[0], (base + r, yz)))
        else:
            each(0, column_rank, lambda r: signal(sems[0], (base + r, yz)))
        for r, y in enumerate(y_order):
            g, q = (y // nyl) * nz * nc + column_rank, (y % nyl) * nx

            @pl.when(r > my_y if later else r < my_y)
            def _():
                for x in range(nx):
                    signal(sems[1], (g, q + x))

        if later:
            each(xx + 1, nx, lambda x: signal(sems[1], (gx, yl * nx + x)))
        else:
            each(0, xx, lambda x: signal(sems[1], (gx, yl * nx + x)))

    okx = (gx > 0, gx < ngx - 1)
    oky = (yz > 0, yz < nyz - 1)
    earlier = [column_rank > 0, column_rank == nz * nc - 1]
    earlier += [y_rank(yh * nyl + div(q, nx)) * nx + mod(q, nx) < my_plane for q in yn]
    mirror = (1, 0, 3, 2)
    ok = okx + oky
    later = [jnp.logical_and(ok[n], jnp.logical_not(earlier[n])) for n in range(4)]
    earlier = [jnp.logical_and(ok[n], earlier[n]) for n in range(4)]
    loads = [pltpu.make_async_copy(s, d, in_sem.at[i])
             for i, (s, d) in enumerate(((e_hbm, E), (p_hbm, PT), (m_hbm, M), (b_hbm, B)))]
    for c in loads:
        c.start()
    barrier = pltpu.get_barrier_semaphore()
    count = column_rank + my_plane
    for n, dev in enumerate(near):
        pl.when(later[n])(functools.partial(signal, barrier, dev))
        count = count + jnp.where(earlier[n], 1, 0)
    group_signals((barrier, barrier), True)

    lane = lax.broadcasted_iota(jnp.int32, (8, lanes), 1)
    sub = lax.broadcasted_iota(jnp.int32, (8, lanes), 0)
    ends, seconds = (0, planes - 1), (1, planes - 2)
    rends, rseconds = (0, rows - 1), (1, rows - 2)

    def at(j):
        return slice(8 * j, 8 * j + 8)

    def below(j):
        return slice(8 * j + 1, 8 * j + 9)

    def before(ref, p, j):
        if j == 0:
            return pltpu.roll(ref[p, at(0), :], 1, 0)
        return ref[p, 8 * j - 1:8 * j + 7, :]

    def after(ref, p, j):
        if j == tiles - 1:
            return pltpu.roll(ref[p, at(j), :], 7, 0)
        return ref[p, below(j), :]

    def right_face(e):
        return jnp.where(lane == lanes - 1, 0.0, face(e, pltpu.roll(e, lanes - 1, 1)))

    def along_z(c, v):
        return c * pltpu.roll(v, lanes - 1, 1) + pltpu.roll(c * v, 1, 1)

    for n in range(4):
        @pl.when(jnp.logical_not(ok[n]))
        def _():
            for ref in ((XB, RB) if n < 2 else (YB,)):
                ref[n % 2] = jnp.ones(ref.shape[1:], f32)

    EX[...] = jnp.ones(EX.shape, f32)
    CY[:, rows:rows + 8, :] = jnp.zeros((planes, 8, lanes), f32)
    CYH[:, rows:rows + 8, :] = jnp.zeros((2, 8, lanes), f32)

    @pl.when(count > 0)
    def _():
        pl.semaphore_wait(barrier, count)

    for n, dev in enumerate(near):
        pl.when(earlier[n])(functools.partial(signal, close.at[mirror[n]], dev))

    loads[0].wait()
    for p in range(planes):
        for j in range(tiles):
            e = E[p, at(j), :]
            CZ[p, at(j), :] = right_face(e)
            cy = face(e, before(E, p, j))
            CY[p, at(j), :] = jnp.where(sub == 0, 0.0, cy) if j == 0 else cy
            if p < planes - 1:
                CX[p, at(j), :] = face(e, E[p + 1, at(j), :])
    loads[1].wait()
    loads[2].wait()
    for p in range(planes):
        for j in range(tiles):
            e, cz = E[p, at(j), :], CZ[p, at(j), :]
            pt = PT[p, at(j), :]
            d = 0.25 * M[p, at(j), :].astype(f32) * (jnp.exp(pt) + jnp.exp(-pt))
            d = d + cz + pltpu.roll(cz, 1, 1) + jnp.where((lane == 0) | (lane == lanes - 1), e, 0.0)
            d = d + CY[p, at(j), :] + CY[p, below(j), :]
            if p > 0:
                d = d + CX[p - 1, at(j), :]
            if p < planes - 1:
                d = d + CX[p, at(j), :]
            D0[p, at(j), :] = d
    loads[3].wait()
    for k in range(2):
        for j in range(tiles):
            TS[k, at(j), :] = (CX[0 if k == 0 else planes - 2, at(j), :] * B[seconds[k], at(j), :]
                               / D0[seconds[k], at(j), :])
        for n, ref in enumerate((E, B, D0)):
            for m in range(2):
                RS[k, 2 * n + m:2 * n + m + 1, :] = ref[seconds[k], rends[m]:rends[m] + 1, :]
            YS[k, n] = ref[:, rends[k], :]
            YS[k, 3 + n] = ref[:, rseconds[k], :]

    group_signals((here.at[0], here.at[1]), False)
    plan = [[] for _ in near]
    for k in range(2):
        plan[2 + k].append((YS.at[k], YB.at[1 - k]))
        for n, ref in enumerate((E, B, D0, TS)):
            plan[k].append((ref.at[k] if n == 3 else ref.at[ends[k]], XB.at[1 - k, n]))
        plan[k].append((RS.at[k], RB.at[1 - k]))
    total, sent = 0, [[] for _ in near]
    for n, dev in enumerate(near):
        for src, dst in plan[n]:
            sent[n].append(pltpu.make_async_remote_copy(
                src_ref=src, dst_ref=dst, send_sem=hs_sem.at[total], recv_sem=hr_sem.at[total],
                device_id=dev, device_id_type=MESH))
            total += 1
    order = (2, 3, 1, 0)

    def send(n):
        for c in sent[n][:4]:
            c.start()

    def send_later(n):
        pl.semaphore_wait(close.at[n], 1)
        send(n)

    for n in order:
        pl.when(earlier[n])(functools.partial(send, n))
    for n in order[:3]:
        pl.when(later[n])(functools.partial(send_later, n))

    for n in (2, 3):
        pl.when(ok[mirror[n]])(sent[n][0].wait_recv)
    for k in range(2):
        for m in range(2):
            for n, (row, p) in enumerate(((0, ends[k]), (1, ends[k]), (2, ends[k]), (0, seconds[k]), (3, ends[k]))):
                RS[k, 6 + 5 * m + n:7 + 5 * m + n, :] = YB[m, row, p:p + 1, :]
    pl.when(ok[1])(sent[1][4].start)

    @pl.when(later[0])
    def _():
        pl.semaphore_wait(close.at[0], 1)

    pl.when(ok[0])(sent[0][4].start)
    pl.when(later[0])(functools.partial(send, 0))
    for n in (1, 0):
        @pl.when(ok[mirror[n]])
        def _():
            for c in (*sent[n][:3], sent[n][4]):
                c.wait_recv()

    last = planes + 1
    for m in range(2):
        for n, (row, corner) in enumerate(((0, 0), (1, 1), (2, 2), (3, 4), (4, None), (5, None))):
            EX[m, n, 1:last, :] = YB[m, row]
            if corner is not None:
                EX[m, n, 0:1, :] = RB[0, 6 + 5 * m + corner:7 + 5 * m + corner, :]
                EX[m, n, last:last + 1, :] = RB[1, 6 + 5 * m + corner:7 + 5 * m + corner, :]
        EX[m, 6, 0:1, :] = XB[0, 0, rends[m]:rends[m] + 1, :]
        EX[m, 6, 1:last, :] = E[:, rends[m], :]
        EX[m, 6, last:last + 1, :] = XB[1, 0, rends[m]:rends[m] + 1, :]
        e1, b1, p1, e2, b2, p2, e0 = (EX[m, n] for n in range(7))

        def crossing(e, outer):
            lo = face(e, pltpu.roll(e, 1, 0))
            hi = pltpu.roll(lo, 7, 0)
            a_lo, a_hi = jnp.where(okx[0], lo, e), jnp.where(okx[1], hi, e)
            add = jnp.where(sub == 1, a_lo, 0.0) + jnp.where(sub == last - 1, a_hi, 0.0)
            if outer:
                add = add + jnp.where(sub == 0, jnp.where(okx[0], hi, e), 0.0)
                add = add + jnp.where(sub == last, jnp.where(okx[1], lo, e), 0.0)
            return lo, add

        lo, add = crossing(e1, True)
        lo = jnp.where(sub == 1, jnp.where(okx[0], lo, 0.0), lo)
        lo = jnp.where(sub == last, jnp.where(okx[1], lo, 0.0), lo)
        fy = face(e1, e0)
        cy = jnp.where(oky[m], fy, 0.0)
        r1 = 1.0 / (p1 + add + jnp.where(oky[m], fy, e1))
        z1 = b1 * r1
        t = face(e1, e2) * b2 / (p2 + crossing(e2, False)[1])
        t = t + along_z(right_face(e1), z1)
        t = t + lo * pltpu.roll(z1, 1, 0) + pltpu.roll(lo, 7, 0) * pltpu.roll(z1, 7, 0)
        ADD[m] = jnp.where(oky[m], fy, e0)
        CY1[m], Z1[m], R1[m], N1[m], PZ[m] = cy, z1, r1, t, cy * z1
        for k in range(2):
            T2[k, 0, m:m + 1, :] = XB[k, 0, rends[m]:rends[m] + 1, :]
            T2[k, 1, m:m + 1, :] = RB[k, 9 + 5 * m:10 + 5 * m, :]
    for k in range(2):
        e1, ed = T2[k, 0], T2[k, 1]
        e2, b2, d2 = RB[k, 0:2, :], RB[k, 2:4, :], RB[k, 4:6, :]
        f = face(e2, ed)
        row2 = lax.broadcasted_iota(jnp.int32, (2, lanes), 0)
        f = jnp.where(row2 == 0, jnp.where(oky[0], f, e2), jnp.where(oky[1], f, e2))
        T4[k] = face(e1, e2) * b2 / (d2 + f)

    def end_rows(j, p1, ref, k0=0):
        t = 0.0
        if j == 0:
            t = t + jnp.where(sub == 0, ref[0, p1:p1 + 1, :], 0.0)
        if j == tiles - 1:
            t = t + jnp.where(sub == 7, ref[1, p1:p1 + 1, :], 0.0)
        return t

    for k, p in enumerate(ends):
        h = last * k
        for j in range(tiles):
            e, eh = E[p, at(j), :], XB[k, 0, at(j), :]
            fx = face(e, eh)
            CXE[k, at(j), :] = jnp.where(okx[k], fx, 0.0)
            d = D0[p, at(j), :] + jnp.where(okx[k], fx, e)
            dh = XB[k, 2, at(j), :] + jnp.where(okx[k], fx, eh)
            if j in (0, tiles - 1):
                d = d + end_rows(j, p + 1, ADD)
                dh = dh + end_rows(j, h, ADD)
            rd, rh = 1.0 / d, 1.0 / dh
            D[p, at(j), :] = d
            RD[p, at(j), :] = rd
            Z[p, at(j), :] = B[p, at(j), :] * rd
            RH[k, at(j), :] = rh
            ZH[k, at(j), :] = XB[k, 1, at(j), :] * rh
            CZH[k, at(j), :] = right_face(eh)
            cy = face(eh, before(XB.at[k], 0, j))
            CYH[k, at(j), :] = jnp.where(sub == 0, 0.0, cy) if j == 0 else cy
    for p in range(1, planes - 1):
        for j in range(tiles):
            d = D0[p, at(j), :]
            if j in (0, tiles - 1):
                d = d + end_rows(j, p + 1, ADD)
            rd = 1.0 / d
            D[p, at(j), :] = d
            RD[p, at(j), :] = rd
            Z[p, at(j), :] = B[p, at(j), :] * rd

    def image(V, VH, PV, p, j):
        v = V[p, at(j), :]
        t = D[p, at(j), :] * v - along_z(CZ[p, at(j), :], v)
        t = t - CY[p, at(j), :] * before(V, p, j) - CY[p, below(j), :] * after(V, p, j)
        if p > 0:
            t = t - CX[p - 1, at(j), :] * V[p - 1, at(j), :]
        else:
            t = t - CXE[0, at(j), :] * VH[0, at(j), :]
        if p < planes - 1:
            t = t - CX[p, at(j), :] * V[p + 1, at(j), :]
        else:
            t = t - CXE[1, at(j), :] * VH[1, at(j), :]
        if j in (0, tiles - 1):
            t = t - end_rows(j, p + 1, PV)
        return t

    s0 = s1 = s2 = s3 = jnp.zeros((8, lanes), f32)
    for p in range(planes):
        for j in range(tiles):
            z = Z[p, at(j), :]
            q = image(Z, ZH, PZ, p, j)
            u = q * RD[p, at(j), :]
            Q[p, at(j), :] = q
            U[p, at(j), :] = u
            s0 = s0 + B[p, at(j), :] * z
            s1 = s1 + z * q
            s2 = s2 + q * u
    for m in range(2):
        EX[m, 7, 1:last, :] = Z[:, rends[m], :]
        t = N1[m] + CY1[m] * EX[m, 7]
        PU[m] = CY1[m] * (Z1[m] - t * R1[m])
    for n in range(2):
        pl.when(ok[mirror[n]])(sent[n][3].wait_recv)
    for k, p in enumerate(ends):
        h = last * k
        for j in range(tiles):
            v = ZH[k, at(j), :]
            t = XB[k, 3, at(j), :]
            if j == 0:
                t = jnp.where(sub == 0, T4[k, 0:1, :], t)
            if j == tiles - 1:
                t = jnp.where(sub == 7, T4[k, 1:2, :], t)
            t = t + CXE[k, at(j), :] * Z[p, at(j), :] + along_z(CZH[k, at(j), :], v)
            t = t + CYH[k, at(j), :] * before(ZH, k, j) + CYH[k, below(j), :] * after(ZH, k, j)
            if j in (0, tiles - 1):
                t = t + end_rows(j, h, PZ)
            UH[k, at(j), :] = v - t * RH[k, at(j), :]
    for p in range(planes):
        for j in range(tiles):
            w = image(U, UH, PU, p, j)
            W[p, at(j), :] = w
            s3 = s3 + U[p, at(j), :] * w

    def folded(s):
        t = s[:, :128]
        for i in range(128, lanes, 128):
            t = t + s[:, i:i + 128]
        return jnp.sum(t, axis=0, keepdims=True)

    lane1 = lax.broadcasted_iota(jnp.int32, (1, 128), 1)
    message = jnp.zeros((1, 128), f32)
    for k, t in enumerate((s0, s1, s2, s3)):
        t = folded(t)
        t = t + pltpu.roll(t, 64, 1)
        t = t + pltpu.roll(t, 32, 1)
        message = jnp.where(lane1 // 32 == k, t, message)
    part[0] = message
    for n, ((peers, got), (size, rank)) in enumerate(zip(stages, sizes_ranks)):
        @pl.when(rank < size - 1)
        def _():
            pl.semaphore_wait(here.at[n], size - 1 - rank)

        for d, dev in enumerate(peers):
            pltpu.make_async_remote_copy(src_ref=part.at[n], dst_ref=got.at[d], send_sem=as_sem.at[n],
                                         recv_sem=ar_sem.at[n], device_id=dev, device_id_type=MESH).start()
        total = part[n]
        if peers:
            pltpu.make_async_copy(got, got, ar_sem.at[n]).wait()
            for d in range(len(peers)):
                total = total + got[d]
        part[n + 1] = total
    row4 = lax.broadcasted_iota(jnp.int32, (4, 128), 0)
    lane4 = lax.broadcasted_iota(jnp.int32, (4, 128), 1)
    s = jnp.sum(jnp.where(lane4 // 32 == row4, part[2], 0.0), axis=1, keepdims=True)
    s0, s1, s2, s3 = s[0:1], s[1:2], s[2:3], s[3:4]
    a, g, h = s0 / s1, s2 / s1, s3 / s1
    cu = (a * g - 1.0) / (h - g * g)
    cz = a + g * cu
    coef[0:1, :] = jnp.broadcast_to(cz, (1, 128))
    coef[1:2, :] = jnp.broadcast_to(cu, (1, 128))
    for n, (peers, got) in enumerate(stages):
        if peers:
            pltpu.make_async_copy(got, got, as_sem.at[n]).wait()
    for n in range(4):
        @pl.when(ok[n])
        def _():
            for c in sent[n]:
                c.wait_send()


def local(sizes, right_side, potential, permittivity, ion_mask):
    f32 = jnp.float32
    planes, rows, lanes = block = right_side.shape
    columns, in_plane = sizes["z"] * sizes["core"], sizes["x"] * sizes["y_hi"] * sizes["y_lo"]
    vm = lambda *s: pltpu.VMEM(s, f32)
    full, pad = vm(*block), vm(2, 8, lanes)
    side = vm(2, rows, lanes)
    scratch = [
        full, full, pltpu.VMEM(block, jnp.int32),
        vm(planes - 1, rows, lanes), side, vm(planes, rows + 8, lanes), full, full, full, full, side,
        vm(2, 4, rows, lanes), vm(2, 16, lanes), vm(2, 6, planes, lanes), vm(2, 16, lanes), vm(2, 6, planes, lanes),
        vm(2, 8, 8, lanes), vm(2, 2, 2, lanes), vm(2, 2, lanes),
        vm(2, rows + 8, lanes), side, side, side, side, pad, pad, pad, pad, pad, pad, pad,
        vm(3, 1, 128), vm(max(columns - 1, 1), 1, 128), vm(max(in_plane - 1, 1), 1, 128),
        pltpu.SemaphoreType.DMA((4,)),
        pltpu.SemaphoreType.DMA((12,)), pltpu.SemaphoreType.DMA((12,)),
        pltpu.SemaphoreType.DMA((2,)), pltpu.SemaphoreType.DMA((2,)), pltpu.SemaphoreType.REGULAR((2,)),
        pltpu.SemaphoreType.REGULAR((4,)),
    ]
    hbm, vmem = pl.BlockSpec(memory_space=pltpu.HBM), pl.BlockSpec(memory_space=pltpu.VMEM)
    args = (right_side, potential, permittivity, ion_mask)
    whole = jax.ShapeDtypeStruct(block, f32)
    fields = pl.pallas_call(
        functools.partial(kernel, sizes),
        out_shape=(whole,) * 5 + (jax.ShapeDtypeStruct((2, 128), f32),),
        in_specs=[hbm] * 4,
        out_specs=(vmem,) * 6,
        scratch_shapes=scratch,
        compiler_params=pltpu.CompilerParams(collective_id=0, has_side_effects=True, vmem_limit_bytes=24 * 2**20),
    )(*[pltpu.with_memory_space_constraint(a, pltpu.HBM) for a in args])
    return pl.pallas_call(
        finish,
        out_shape=(whole, whole),
        in_specs=[vmem] * 6,
        out_specs=(hbm, hbm),
        scratch_shapes=[full, full, pltpu.SemaphoreType.DMA((2, planes))],
        compiler_params=pltpu.CompilerParams(vmem_limit_bytes=16 * 2**20),
    )(*fields)


def finish(B, Z, U, Q, W, coef, x_out, r_out, X, R, sem):
    cz, cu = coef[0:1, 0:1], coef[1:2, 0:1]
    stores = []
    for p in range(B.shape[0]):
        X[p] = cz * Z[p] - cu * U[p]
        R[p] = B[p] - cz * Q[p] + cu * W[p]
        for i, (src, dst) in enumerate(((X, x_out), (R, r_out))):
            c = pltpu.make_async_copy(src.at[p], dst.at[p], sem.at[i, p])
            c.start()
            stores.append(c)
    for c in stores:
        c.wait()


def solution(mesh, sizes=SIZES):
    spec = P("gx", "yz", None)
    return jax.shard_map(functools.partial(local, sizes), mesh=mesh, in_specs=(spec,) * 4, out_specs=(spec,) * 2,
                         check_vma=False)
```

```python
import functools

import jax
import jax.numpy as jnp
from jax import lax
from jax.experimental import pallas as pl
from jax.experimental.pallas import tpu as pltpu
from jax.sharding import PartitionSpec as P

MESH = pl.DeviceIdType.MESH
SIZES = dict(y_hi=4, z=12, core=2, y_lo=2, x=4)


def face(a, b):
    return (2.0 * a * b) / (a + b)


def div(a, n):
    return a >> (n.bit_length() - 1) if n & (n - 1) == 0 else lax.div(a, jnp.int32(n))


def mod(a, n):
    return a & (n - 1) if n & (n - 1) == 0 else a - div(a, n) * n


def kernel(sizes, b_hbm, p_hbm, e_hbm, m_hbm, B, Z, U, Q, W, coef,
           PT, E, M, CX, CXE, CY, CZ, D0, D, RD, TS,
           XB, RB, YB, RS, YS, EX, T2, T4, CYH, CZH, ZH, RH, UH, ADD, CY1, Z1, R1, N1, PZ, PU,
           part, g0, g1, in_sem, hs_sem, hr_sem, as_sem, ar_sem, here, close):
    nyh, nz, nc, nyl, nx = (sizes[k] for k in ("y_hi", "z", "core", "y_lo", "x"))
    ngx, nyz = nyh * nz * nc, nyl * nx
    gx, yz = lax.axis_index("gx"), lax.axis_index("yz")
    core, yh = mod(gx, nc), div(gx, nz * nc)
    zz = div(gx - yh * (nz * nc), nc)
    xx, yl = mod(yz, nx), div(yz, nx)
    ny = nyh * nyl
    yy = yh * nyl + yl
    planes, rows, lanes = E.shape
    tiles = rows // 8
    f32 = jnp.float32

    def wrap(a, n):
        return jnp.where(a >= n, a - n, a)

    xn = (jnp.where(gx > 0, gx, ngx) - 1, wrap(gx + 1, ngx))
    yn = (jnp.where(yz > 0, yz, nyz) - 1, wrap(yz + 1, nyz))
    near = [(xn[k], yz) for k in range(2)] + [(gx, yn[k]) for k in range(2)]

    def place(y, z, c, x):
        return ((div(y, nyl) * nz + z) * nc + c, mod(y, nyl) * nx + x)

    def y_rank(y):
        return jnp.where(y == 0, 0, jnp.where(2 * y <= ny, 2 * y - 1, 2 * (ny - y)))

    column_rank, my_y = zz * nc + core, y_rank(yy)
    my_plane = my_y * nx + xx
    y_order = sorted(range(ny), key=lambda y: min(y, ny - y) * 2 + (2 * y > ny))
    sizes_ranks = ((nz * nc, column_rank), (ny * nx, my_plane))

    def far(a, n):
        return min(a, n - a)

    offsets = sorted(((a, b) for a in range(ny) for b in range(nx) if a or b), key=lambda o: -far(o[0], ny) - far(o[1], nx))
    plane_peers = [place(wrap(yy + a, ny), zz, core, wrap(xx + b, nx)) for a, b in offsets]
    column_peers = [place(yy, wrap(zz + a, nz), wrap(core + b, nc), xx) for a in range(nz) for b in range(nc) if a or b]
    stages = ((column_peers, g0), (plane_peers, g1))

    def signal(sem, dev):
        pl.semaphore_signal(sem, inc=1, device_id=dev, device_id_type=MESH)

    def each(start, stop, act):
        lax.fori_loop(start, stop, lambda i, c: (act(i), c)[1], 0)

    def group_signals(sems, later):
        base = gx - column_rank
        if later:
            each(column_rank + 1, nz * nc, lambda r: signal(sems[0], (base + r, yz)))
        else:
            each(0, column_rank, lambda r: signal(sems[0], (base + r, yz)))
        for r, y in enumerate(y_order):
            g, q = (y // nyl) * nz * nc + column_rank, (y % nyl) * nx

            @pl.when(r > my_y if later else r < my_y)
            def _():
                for x in range(nx):
                    signal(sems[1], (g, q + x))

        if later:
            each(xx + 1, nx, lambda x: signal(sems[1], (gx, yl * nx + x)))
        else:
            each(0, xx, lambda x: signal(sems[1], (gx, yl * nx + x)))

    okx = (gx > 0, gx < ngx - 1)
    oky = (yz > 0, yz < nyz - 1)
    earlier = [column_rank > 0, column_rank == nz * nc - 1]
    earlier += [y_rank(yh * nyl + div(q, nx)) * nx + mod(q, nx) < my_plane for q in yn]
    mirror = (1, 0, 3, 2)
    ok = okx + oky
    later = [jnp.logical_and(ok[n], jnp.logical_not(earlier[n])) for n in range(4)]
    earlier = [jnp.logical_and(ok[n], earlier[n]) for n in range(4)]
    loads = [pltpu.make_async_copy(s, d, in_sem.at[i])
             for i, (s, d) in enumerate(((e_hbm, E), (p_hbm, PT), (m_hbm, M), (b_hbm, B)))]
    for c in loads:
        c.start()
    barrier = pltpu.get_barrier_semaphore()
    count = column_rank + my_plane
    for n, dev in enumerate(near):
        pl.when(later[n])(functools.partial(signal, barrier, dev))
        count = count + jnp.where(earlier[n], 1, 0)
    group_signals((barrier, barrier), True)

    lane = lax.broadcasted_iota(jnp.int32, (8, lanes), 1)
    sub = lax.broadcasted_iota(jnp.int32, (8, lanes), 0)
    ends, seconds = (0, planes - 1), (1, planes - 2)
    rends, rseconds = (0, rows - 1), (1, rows - 2)

    def at(j):
        return slice(8 * j, 8 * j + 8)

    def below(j):
        return slice(8 * j + 1, 8 * j + 9)

    def before(ref, p, j):
        if j == 0:
            return pltpu.roll(ref[p, at(0), :], 1, 0)
        return ref[p, 8 * j - 1:8 * j + 7, :]

    def after(ref, p, j):
        if j == tiles - 1:
            return pltpu.roll(ref[p, at(j), :], 7, 0)
        return ref[p, below(j), :]

    def right_face(e):
        return jnp.where(lane == lanes - 1, 0.0, face(e, pltpu.roll(e, lanes - 1, 1)))

    def along_z(c, v):
        return c * pltpu.roll(v, lanes - 1, 1) + pltpu.roll(c * v, 1, 1)

    for n in range(4):
        @pl.when(jnp.logical_not(ok[n]))
        def _():
            for ref in ((XB, RB) if n < 2 else (YB,)):
                ref[n % 2] = jnp.ones(ref.shape[1:], f32)

    EX[...] = jnp.ones(EX.shape, f32)
    CY[:, rows:rows + 8, :] = jnp.zeros((planes, 8, lanes), f32)
    CYH[:, rows:rows + 8, :] = jnp.zeros((2, 8, lanes), f32)

    @pl.when(count > 0)
    def _():
        pl.semaphore_wait(barrier, count)

    for n, dev in enumerate(near):
        pl.when(earlier[n])(functools.partial(signal, close.at[mirror[n]], dev))

    group_signals((here.at[0], here.at[1]), False)

    loads[0].wait()
    for p in range(planes):
        for j in range(tiles):
            e = E[p, at(j), :]
            CZ[p, at(j), :] = right_face(e)
            cy = face(e, before(E, p, j))
            CY[p, at(j), :] = jnp.where(sub == 0, 0.0, cy) if j == 0 else cy
            if p < planes - 1:
                CX[p, at(j), :] = face(e, E[p + 1, at(j), :])
    loads[1].wait()
    loads[2].wait()
    for p in range(planes):
        for j in range(tiles):
            e, cz = E[p, at(j), :], CZ[p, at(j), :]
            pt = PT[p, at(j), :]
            d = 0.25 * M[p, at(j), :].astype(f32) * (jnp.exp(pt) + jnp.exp(-pt))
            d = d + cz + pltpu.roll(cz, 1, 1) + jnp.where((lane == 0) | (lane == lanes - 1), e, 0.0)
            d = d + CY[p, at(j), :] + CY[p, below(j), :]
            if p > 0:
                d = d + CX[p - 1, at(j), :]
            if p < planes - 1:
                d = d + CX[p, at(j), :]
            D0[p, at(j), :] = d
    loads[3].wait()
    for k in range(2):
        for j in range(tiles):
            TS[k, at(j), :] = (CX[0 if k == 0 else planes - 2, at(j), :] * B[seconds[k], at(j), :]
                               / D0[seconds[k], at(j), :])
        for n, ref in enumerate((E, B, D0)):
            for m in range(2):
                RS[k, 2 * n + m:2 * n + m + 1, :] = ref[seconds[k], rends[m]:rends[m] + 1, :]
            YS[k, n] = ref[:, rends[k], :]
            YS[k, 3 + n] = ref[:, rseconds[k], :]

    plan = [[] for _ in near]
    for k in range(2):
        plan[2 + k].append((YS.at[k], YB.at[1 - k]))
        for n, ref in enumerate((E, B, D0, TS)):
            plan[k].append((ref.at[k] if n == 3 else ref.at[ends[k]], XB.at[1 - k, n]))
        plan[k].append((RS.at[k], RB.at[1 - k]))
    total, sent = 0, [[] for _ in near]
    for n, dev in enumerate(near):
        for src, dst in plan[n]:
            sent[n].append(pltpu.make_async_remote_copy(
                src_ref=src, dst_ref=dst, send_sem=hs_sem.at[total], recv_sem=hr_sem.at[total],
                device_id=dev, device_id_type=MESH))
            total += 1
    order = (2, 3, 1, 0)

    def send(n):
        for c in sent[n][:4]:
            c.start()

    def send_later(n):
        pl.semaphore_wait(close.at[n], 1)
        send(n)

    for n in order:
        pl.when(earlier[n])(functools.partial(send, n))
    for n in order[:3]:
        pl.when(later[n])(functools.partial(send_later, n))

    for n in (2, 3):
        pl.when(ok[mirror[n]])(sent[n][0].wait_recv)
    for k in range(2):
        for m in range(2):
            for n, (row, p) in enumerate(((0, ends[k]), (1, ends[k]), (2, ends[k]), (0, seconds[k]), (3, ends[k]))):
                RS[k, 6 + 5 * m + n:7 + 5 * m + n, :] = YB[m, row, p:p + 1, :]
    pl.when(ok[1])(sent[1][4].start)

    @pl.when(later[0])
    def _():
        pl.semaphore_wait(close.at[0], 1)

    pl.when(ok[0])(sent[0][4].start)
    pl.when(later[0])(functools.partial(send, 0))
    for n in (1, 0):
        @pl.when(ok[mirror[n]])
        def _():
            for c in (*sent[n][:3], sent[n][4]):
                c.wait_recv()

    last = planes + 1
    for m in range(2):
        for n, (row, corner) in enumerate(((0, 0), (1, 1), (2, 2), (3, 4), (4, None), (5, None))):
            EX[m, n, 1:last, :] = YB[m, row]
            if corner is not None:
                EX[m, n, 0:1, :] = RB[0, 6 + 5 * m + corner:7 + 5 * m + corner, :]
                EX[m, n, last:last + 1, :] = RB[1, 6 + 5 * m + corner:7 + 5 * m + corner, :]
        EX[m, 6, 0:1, :] = XB[0, 0, rends[m]:rends[m] + 1, :]
        EX[m, 6, 1:last, :] = E[:, rends[m], :]
        EX[m, 6, last:last + 1, :] = XB[1, 0, rends[m]:rends[m] + 1, :]
        e1, b1, p1, e2, b2, p2, e0 = (EX[m, n] for n in range(7))

        def crossing(e, outer):
            lo = face(e, pltpu.roll(e, 1, 0))
            hi = pltpu.roll(lo, 7, 0)
            a_lo, a_hi = jnp.where(okx[0], lo, e), jnp.where(okx[1], hi, e)
            add = jnp.where(sub == 1, a_lo, 0.0) + jnp.where(sub == last - 1, a_hi, 0.0)
            if outer:
                add = add + jnp.where(sub == 0, jnp.where(okx[0], hi, e), 0.0)
                add = add + jnp.where(sub == last, jnp.where(okx[1], lo, e), 0.0)
            return lo, add

        lo, add = crossing(e1, True)
        lo = jnp.where(sub == 1, jnp.where(okx[0], lo, 0.0), lo)
        lo = jnp.where(sub == last, jnp.where(okx[1], lo, 0.0), lo)
        fy = face(e1, e0)
        cy = jnp.where(oky[m], fy, 0.0)
        r1 = 1.0 / (p1 + add + jnp.where(oky[m], fy, e1))
        z1 = b1 * r1
        t = face(e1, e2) * b2 / (p2 + crossing(e2, False)[1])
        t = t + along_z(right_face(e1), z1)
        t = t + lo * pltpu.roll(z1, 1, 0) + pltpu.roll(lo, 7, 0) * pltpu.roll(z1, 7, 0)
        ADD[m] = jnp.where(oky[m], fy, e0)
        CY1[m], Z1[m], R1[m], N1[m], PZ[m] = cy, z1, r1, t, cy * z1
        for k in range(2):
            T2[k, 0, m:m + 1, :] = XB[k, 0, rends[m]:rends[m] + 1, :]
            T2[k, 1, m:m + 1, :] = RB[k, 9 + 5 * m:10 + 5 * m, :]
    for k in range(2):
        e1, ed = T2[k, 0], T2[k, 1]
        e2, b2, d2 = RB[k, 0:2, :], RB[k, 2:4, :], RB[k, 4:6, :]
        f = face(e2, ed)
        row2 = lax.broadcasted_iota(jnp.int32, (2, lanes), 0)
        f = jnp.where(row2 == 0, jnp.where(oky[0], f, e2), jnp.where(oky[1], f, e2))
        T4[k] = face(e1, e2) * b2 / (d2 + f)

    def end_rows(j, p1, ref, k0=0):
        t = 0.0
        if j == 0:
            t = t + jnp.where(sub == 0, ref[0, p1:p1 + 1, :], 0.0)
        if j == tiles - 1:
            t = t + jnp.where(sub == 7, ref[1, p1:p1 + 1, :], 0.0)
        return t

    for k, p in enumerate(ends):
        h = last * k
        for j in range(tiles):
            e, eh = E[p, at(j), :], XB[k, 0, at(j), :]
            fx = face(e, eh)
            CXE[k, at(j), :] = jnp.where(okx[k], fx, 0.0)
            d = D0[p, at(j), :] + jnp.where(okx[k], fx, e)
            dh = XB[k, 2, at(j), :] + jnp.where(okx[k], fx, eh)
            if j in (0, tiles - 1):
                d = d + end_rows(j, p + 1, ADD)
                dh = dh + end_rows(j, h, ADD)
            rd, rh = 1.0 / d, 1.0 / dh
            D[p, at(j), :] = d
            RD[p, at(j), :] = rd
            Z[p, at(j), :] = B[p, at(j), :] * rd
            RH[k, at(j), :] = rh
            ZH[k, at(j), :] = XB[k, 1, at(j), :] * rh
            CZH[k, at(j), :] = right_face(eh)
            cy = face(eh, before(XB.at[k], 0, j))
            CYH[k, at(j), :] = jnp.where(sub == 0, 0.0, cy) if j == 0 else cy
    for p in range(1, planes - 1):
        for j in range(tiles):
            d = D0[p, at(j), :]
            if j in (0, tiles - 1):
                d = d + end_rows(j, p + 1, ADD)
            rd = 1.0 / d
            D[p, at(j), :] = d
            RD[p, at(j), :] = rd
            Z[p, at(j), :] = B[p, at(j), :] * rd

    def image(V, VH, PV, p, j):
        v = V[p, at(j), :]
        t = D[p, at(j), :] * v - along_z(CZ[p, at(j), :], v)
        t = t - CY[p, at(j), :] * before(V, p, j) - CY[p, below(j), :] * after(V, p, j)
        if p > 0:
            t = t - CX[p - 1, at(j), :] * V[p - 1, at(j), :]
        else:
            t = t - CXE[0, at(j), :] * VH[0, at(j), :]
        if p < planes - 1:
            t = t - CX[p, at(j), :] * V[p + 1, at(j), :]
        else:
            t = t - CXE[1, at(j), :] * VH[1, at(j), :]
        if j in (0, tiles - 1):
            t = t - end_rows(j, p + 1, PV)
        return t

    s0 = s1 = s2 = s3 = jnp.zeros((8, lanes), f32)
    for p in range(planes):
        for j in range(tiles):
            z = Z[p, at(j), :]
            q = image(Z, ZH, PZ, p, j)
            u = q * RD[p, at(j), :]
            Q[p, at(j), :] = q
            U[p, at(j), :] = u
            s0 = s0 + B[p, at(j), :] * z
            s1 = s1 + z * q
            s2 = s2 + q * u
    for m in range(2):
        EX[m, 7, 1:last, :] = Z[:, rends[m], :]
        t = N1[m] + CY1[m] * EX[m, 7]
        PU[m] = CY1[m] * (Z1[m] - t * R1[m])
    for n in range(2):
        pl.when(ok[mirror[n]])(sent[n][3].wait_recv)
    for k, p in enumerate(ends):
        h = last * k
        for j in range(tiles):
            v = ZH[k, at(j), :]
            t = XB[k, 3, at(j), :]
            if j == 0:
                t = jnp.where(sub == 0, T4[k, 0:1, :], t)
            if j == tiles - 1:
                t = jnp.where(sub == 7, T4[k, 1:2, :], t)
            t = t + CXE[k, at(j), :] * Z[p, at(j), :] + along_z(CZH[k, at(j), :], v)
            t = t + CYH[k, at(j), :] * before(ZH, k, j) + CYH[k, below(j), :] * after(ZH, k, j)
            if j in (0, tiles - 1):
                t = t + end_rows(j, h, PZ)
            UH[k, at(j), :] = v - t * RH[k, at(j), :]
    for p in range(planes):
        for j in range(tiles):
            w = image(U, UH, PU, p, j)
            W[p, at(j), :] = w
            s3 = s3 + U[p, at(j), :] * w

    def folded(s):
        t = s[:, :128]
        for i in range(128, lanes, 128):
            t = t + s[:, i:i + 128]
        return jnp.sum(t, axis=0, keepdims=True)

    lane1 = lax.broadcasted_iota(jnp.int32, (1, 128), 1)
    message = jnp.zeros((1, 128), f32)
    for k, t in enumerate((s0, s1, s2, s3)):
        t = folded(t)
        t = t + pltpu.roll(t, 64, 1)
        t = t + pltpu.roll(t, 32, 1)
        message = jnp.where(lane1 // 32 == k, t, message)
    part[0] = message
    for n, ((peers, got), (size, rank)) in enumerate(zip(stages, sizes_ranks)):
        @pl.when(rank < size - 1)
        def _():
            pl.semaphore_wait(here.at[n], size - 1 - rank)

        for d, dev in enumerate(peers):
            pltpu.make_async_remote_copy(src_ref=part.at[n], dst_ref=got.at[d], send_sem=as_sem.at[n],
                                         recv_sem=ar_sem.at[n], device_id=dev, device_id_type=MESH).start()
        total = part[n]
        if peers:
            pltpu.make_async_copy(got, got, ar_sem.at[n]).wait()
            for d in range(len(peers)):
                total = total + got[d]
        part[n + 1] = total
    row4 = lax.broadcasted_iota(jnp.int32, (4, 128), 0)
    lane4 = lax.broadcasted_iota(jnp.int32, (4, 128), 1)
    s = jnp.sum(jnp.where(lane4 // 32 == row4, part[2], 0.0), axis=1, keepdims=True)
    s0, s1, s2, s3 = s[0:1], s[1:2], s[2:3], s[3:4]
    a, g, h = s0 / s1, s2 / s1, s3 / s1
    cu = (a * g - 1.0) / (h - g * g)
    cz = a + g * cu
    coef[0:1, :] = jnp.broadcast_to(cz, (1, 128))
    coef[1:2, :] = jnp.broadcast_to(cu, (1, 128))
    for n, (peers, got) in enumerate(stages):
        if peers:
            pltpu.make_async_copy(got, got, as_sem.at[n]).wait()
    for n in range(4):
        @pl.when(ok[n])
        def _():
            for c in sent[n]:
                c.wait_send()


def local(sizes, right_side, potential, permittivity, ion_mask):
    f32 = jnp.float32
    planes, rows, lanes = block = right_side.shape
    columns, in_plane = sizes["z"] * sizes["core"], sizes["x"] * sizes["y_hi"] * sizes["y_lo"]
    vm = lambda *s: pltpu.VMEM(s, f32)
    full, pad = vm(*block), vm(2, 8, lanes)
    side = vm(2, rows, lanes)
    scratch = [
        full, full, pltpu.VMEM(block, jnp.int32),
        vm(planes - 1, rows, lanes), side, vm(planes, rows + 8, lanes), full, full, full, full, side,
        vm(2, 4, rows, lanes), vm(2, 16, lanes), vm(2, 6, planes, lanes), vm(2, 16, lanes), vm(2, 6, planes, lanes),
        vm(2, 8, 8, lanes), vm(2, 2, 2, lanes), vm(2, 2, lanes),
        vm(2, rows + 8, lanes), side, side, side, side, pad, pad, pad, pad, pad, pad, pad,
        vm(3, 1, 128), vm(max(columns - 1, 1), 1, 128), vm(max(in_plane - 1, 1), 1, 128),
        pltpu.SemaphoreType.DMA((4,)),
        pltpu.SemaphoreType.DMA((12,)), pltpu.SemaphoreType.DMA((12,)),
        pltpu.SemaphoreType.DMA((2,)), pltpu.SemaphoreType.DMA((2,)), pltpu.SemaphoreType.REGULAR((2,)),
        pltpu.SemaphoreType.REGULAR((4,)),
    ]
    hbm, vmem = pl.BlockSpec(memory_space=pltpu.HBM), pl.BlockSpec(memory_space=pltpu.VMEM)
    args = (right_side, potential, permittivity, ion_mask)
    whole = jax.ShapeDtypeStruct(block, f32)
    fields = pl.pallas_call(
        functools.partial(kernel, sizes),
        out_shape=(whole,) * 5 + (jax.ShapeDtypeStruct((2, 128), f32),),
        in_specs=[hbm] * 4,
        out_specs=(vmem,) * 6,
        scratch_shapes=scratch,
        compiler_params=pltpu.CompilerParams(collective_id=0, has_side_effects=True, vmem_limit_bytes=24 * 2**20),
    )(*[pltpu.with_memory_space_constraint(a, pltpu.HBM) for a in args])
    return pl.pallas_call(
        finish,
        out_shape=(whole, whole),
        in_specs=[vmem] * 6,
        out_specs=(hbm, hbm),
        scratch_shapes=[full, full, pltpu.SemaphoreType.DMA((2, planes))],
        compiler_params=pltpu.CompilerParams(vmem_limit_bytes=16 * 2**20),
    )(*fields)


def finish(B, Z, U, Q, W, coef, x_out, r_out, X, R, sem):
    cz, cu = coef[0:1, 0:1], coef[1:2, 0:1]
    stores = []
    for p in range(B.shape[0]):
        X[p] = cz * Z[p] - cu * U[p]
        R[p] = B[p] - cz * Q[p] + cu * W[p]
        for i, (src, dst) in enumerate(((X, x_out), (R, r_out))):
            c = pltpu.make_async_copy(src.at[p], dst.at[p], sem.at[i, p])
            c.start()
            stores.append(c)
    for c in stores:
        c.wait()


def solution(mesh, sizes=SIZES):
    spec = P("gx", "yz", None)
    return jax.shard_map(functools.partial(local, sizes), mesh=mesh, in_specs=(spec,) * 4, out_specs=(spec,) * 2,
                         check_vma=False)
```
